256 devices in a mesh: dp: 8 (over y, z_hi), mp: 32 (over z_lo, x, core).
Axes of the slice: x: 4, y: 4, z: 8 (z_hi: 2, z_lo: 4; z = z_hi * 4 + z_lo), core: 2. Of those that a mesh axis runs over, the one named last changes fastest.
Arguments:
- responses: bfloat16 [2048, 4608], P('dp', 'mp'), may hold values from -6 to 6
- frozen_weight: bfloat16 [36864, 4608], P('mp'), may hold values from -0.09375 to 0.09375
- skew_param: float32 [2, 1152, 32, 32], P(None, 'mp'), may hold values from -0.6 to 0.6
- section_perm: int32 [2, 32], replicated, may hold values from 0 to 31, each once within a row
- prefix_ids: int32 [2048], P('dp'), may hold values from 0 to 15
- prefix_scale: float32 [16, 36864], P(None, 'mp'), may hold values from 0.1 to 1.9
- out_grad: bfloat16 [36864, 2048], P('mp', 'dp'), may hold values from -6 to 6
Outputs:
- judged: bfloat16 [36864, 2048], P('mp', 'dp')
- input_grad: bfloat16 [4608, 2048], P('mp', 'dp')
- skew_grad: float32 [2, 1152, 32, 32], P(None, 'mp')
The draws below stay inside these ranges and needn't reach their ends.
Inputs may be any that keep to these rules, and one draw needn't show every extreme that they name: `section_perm`: each row is a permutation of 0 to 31.
All inputs are finite; a program needn't handle non-finite values.
Results may differ from the reference program's by a relative error of at most 0.005.
Values may be sent and summed in bfloat16 or wider, within the bound.
No kernel may reach another device: no remote copies, remote signals or barrier semaphores. Data moves between devices by JAX's collectives and lax.ppermute only.
A program may use at most 128 MiB of HBM per device.

```python
import math
import jax
import jax.numpy as jnp
import numpy as np
from jax import lax

D = 4608
OUT = 36864
BLOCK = 32
SECTIONS = 2
PREFIXES = 16
ROWS = 2048
N_MP = 32


def set_ends(entries, stream_key, smallest, top_value):
    index_at = [jax.random.randint(jax.random.fold_in(stream_key, axis), (), 0, length) for axis, length in enumerate(entries.shape)]
    longest = entries.shape.index(max(entries.shape))
    beside = index_at[:longest] + [(index_at[longest] + 1) % entries.shape[longest]] + index_at[longest + 1:]
    return entries.at[tuple(index_at)].set(smallest).at[tuple(beside)].set(top_value)


def shard_levels(key, extent, pieces, smallest, high):
    gain, own = 1.0, jax.random.fold_in(key, 6)
    for dim, blocks in pieces:
        draws = jnp.exp(jax.random.uniform(jax.random.fold_in(own, dim), (blocks,), jnp.float32, smallest / len(pieces), high / len(pieces)))
        gain = gain * jnp.repeat(draws, extent[dim] // blocks).reshape([-1 if axis == dim else 1 for axis in range(len(extent))])
    return gain


def cumulative_ranks(number_of, slope):
    portions = [(1 << 20) // math.isqrt(rank ** slope) + 1 for rank in range(1, number_of + 1)]
    width = 1 + sum(portions) // (1 << 30)
    return np.cumsum(np.array([max(1, weight // width) for weight in portions]))


def skewed_ids(key, dims, count, slope):
    listing = cumulative_ranks(count, slope)
    ticket = jax.random.randint(jax.random.fold_in(key, 1), dims, 0, int(listing[count - 1]))
    standing = jnp.searchsorted(jnp.asarray(listing, jnp.int32), ticket, side="right")
    return jax.random.permutation(jax.random.fold_in(key, 2), count)[standing].astype(jnp.int32)


def normal_values(rng, dims, deviation, most, split=(), kind=jnp.bfloat16):
    values = jax.random.normal(rng, dims, jnp.float32) * deviation
    if len(split) > 0:
        values = shard_levels(rng, dims, split, -0.22, 0.18) * values
    return jnp.clip(values, min=-most, max=most).astype(kind)


def setup_inputs(seed: int = 0) -> dict:
    key_list = jax.random.split(jax.random.key(seed), 8)
    return {
        "responses": normal_values(key_list[0], (ROWS, D), 1.0, 6.0, ((0, 8), (1, 32))),
        "frozen_weight": normal_values(key_list[1], (OUT, D), D ** -0.5, 0.09375, ((0, 32),)),
        "skew_param": normal_values(key_list[2], (SECTIONS, OUT // BLOCK, BLOCK, BLOCK), 0.1, 0.6, ((1, 32),), jnp.float32),
        "section_perm": jax.vmap(lambda own: jax.random.permutation(own, BLOCK))(jax.random.split(key_list[3], SECTIONS)).reshape((SECTIONS, BLOCK)).astype(jnp.int32),
        "prefix_ids": set_ends(skewed_ids(key_list[4], (ROWS,), PREFIXES, 2), jax.random.fold_in(key_list[4], 3), 0, PREFIXES - 1).astype(jnp.int32),
        "prefix_scale": jnp.clip(1.0 + 0.18 * jax.random.normal(key_list[5], (PREFIXES, OUT), jnp.float32), 0.1, 1.9),
        "out_grad": normal_values(key_list[6], (OUT, ROWS), 1.0, 6.0, ((0, 32), (1, 8))),
    }


def rotations(skew_param, section_perm):
    highest = lax.Precision.HIGHEST
    block_width = skew_param.shape[-1]
    skew_part = skew_param - jnp.swapaxes(skew_param, -1, -2)
    identity = jnp.eye(block_width, dtype=jnp.float32)
    minus_part = identity - skew_part
    gram_matrix = identity - jnp.matmul(skew_part, skew_part, precision=highest)
    squared = jnp.matmul(minus_part, minus_part, precision=highest)
    factor = jnp.linalg.cholesky(gram_matrix)
    rotation = jax.scipy.linalg.cho_solve((factor, True), squared)
    select = (section_perm[:, :, None] == jnp.arange(block_width, dtype=jnp.int32)[None, None, :]).astype(jnp.float32)
    return jnp.einsum('sua,sjuw,swc->sjac', select, rotation, select, precision=highest)

def pair_whole(current, span, blocks_dev):
    row_count = current.shape[-1]
    shaped = current.reshape(-1, 2, span, blocks_dev, 2, BLOCK // 2, row_count)
    return jnp.swapaxes(shaped, 1, 4).reshape(-1, BLOCK, row_count)

def unpair_whole(blocks, span, blocks_dev):
    row_count = blocks.shape[-1]
    shaped = blocks.reshape(-1, 2, span, blocks_dev, 2, BLOCK // 2, row_count)
    return jnp.swapaxes(shaped, 1, 4).reshape(-1, row_count)

def reference(responses, frozen_weight, skew_param, section_perm, prefix_ids, prefix_scale, out_grad):
    highest = lax.Precision.HIGHEST
    blocks_dev = OUT // N_MP // BLOCK
    top_bit = N_MP.bit_length() - 1
    rotation = rotations(skew_param, section_perm)
    hidden = jnp.dot(frozen_weight.astype(jnp.float32), responses.T.astype(jnp.float32), preferred_element_type=jnp.float32)
    onehot = (prefix_ids[None, :] == jnp.arange(PREFIXES, dtype=jnp.int32)[:, None]).astype(jnp.float32)
    scale_rows = lax.dot_general(prefix_scale, onehot, (((0,), (0,)), ((), ())), precision=highest)
    current = hidden
    stored = []
    for section in range(SECTIONS):
        span = 2 ** (top_bit - 1 - section)
        blocks = pair_whole(current, span, blocks_dev)
        stored.append(blocks)
        turned = jnp.einsum('bac,bcr->bar', rotation[section], blocks, precision=highest)
        current = unpair_whole(turned, span, blocks_dev)
    judged = (current * scale_rows).astype(jnp.bfloat16)
    adjoint = out_grad.astype(jnp.float32) * scale_rows
    section_grads = [None] * SECTIONS
    for section in reversed(range(SECTIONS)):
        span = 2 ** (top_bit - 1 - section)
        incoming = pair_whole(adjoint, span, blocks_dev)
        section_grads[section] = jnp.einsum('bar,bcr->bac', incoming, stored[section], precision=highest)
        turned = jnp.einsum('bac,bar->bcr', rotation[section], incoming, precision=highest)
        adjoint = unpair_whole(turned, span, blocks_dev)
    rotation_grad = jnp.stack(section_grads) * (1.0 / ROWS ** 0.5)
    unused, pullback = jax.vjp(lambda params: rotations(params, section_perm), skew_param)
    skew_grad = pullback(rotation_grad)[0]
    hidden_grad = adjoint.astype(jnp.bfloat16)
    input_grad = jnp.dot(frozen_weight.T.astype(jnp.float32), hidden_grad.astype(jnp.float32), preferred_element_type=jnp.float32).astype(jnp.bfloat16)
    return (judged, input_grad, skew_grad)
```

```python
import functools

import jax
import jax.numpy as jnp
from jax import lax
from jax.experimental import pallas as pl
from jax.experimental.pallas import tpu as pltpu
from jax.sharding import Mesh, PartitionSpec as P

F32 = jnp.float32
BF16 = jnp.bfloat16
GROUP = 4
VMEM_LIMIT = 56 * 1024 * 1024

VMEM = pl.BlockSpec(memory_space=pltpu.VMEM)
SMEM = pl.BlockSpec(memory_space=pltpu.SMEM)
PARAMS = pltpu.CompilerParams(vmem_limit_bytes=VMEM_LIMIT)


def xor(x, axis, k):
    return lax.ppermute(x, axis, [(i, i ^ k) for i in range(lax.axis_size(axis))])


def shift(x, axis, k):
    n = lax.axis_size(axis)
    return lax.ppermute(x, axis, [(i, (i + k) % n) for i in range(n)])


def mm(a, b):
    return jnp.dot(a, b, preferred_element_type=F32)


def split(x):
    hi = x.astype(BF16)
    return hi, (x - hi.astype(F32)).astype(BF16)


def rot_kernel(k_ref, pi_ref, pot_ref, m_ref, mt_ref, at_ref, raw, mat, turned):
    n = k_ref.shape[1]
    blocks = k_ref.shape[3]
    raw[...] = jnp.zeros_like(raw)
    for s in range(2):
        raw[:, 64 * s : 64 * s + blocks] = k_ref[s].reshape(n * n, blocks)
    sub = lax.broadcasted_iota(jnp.int32, (n, 128), 0)
    for u in range(n):
        mat[u * n : (u + 1) * n, :] = (
            raw[u * n : (u + 1) * n, :] - raw[pl.ds(u, n, stride=n), :]
            + jnp.where(sub == u, 1.0, 0.0)
        )

    def eliminate(k, carry):
        at = sub == k
        base = pl.multiple_of(k * n, n)
        pivot = 1.0 / mat[pl.ds(base + k, 1), :]
        row = jnp.where(at, 1.0, mat[pl.ds(base, n), :]) * pivot
        for i in range(n):
            factor = mat[pl.ds(i * n + k, 1), :]
            mine = jnp.where(at, 0.0, mat[i * n : (i + 1) * n, :])
            mat[i * n : (i + 1) * n, :] = mine - factor * row
        mat[pl.ds(base, n), :] = row
        return carry

    lax.fori_loop(0, n, eliminate, 0)
    for u in range(n):
        turned[u * 128 : (u + 1) * 128, :] = jnp.transpose(mat[u * n : (u + 1) * n, :])
    width = GROUP * n
    r = lax.broadcasted_iota(jnp.int32, (width, width), 0) // n
    c = lax.broadcasted_iota(jnp.int32, (width, width), 1) // n
    diagonal = r == c
    for s in range(2):
        pi, pot = pi_ref[s], pot_ref[s]
        ident = mm(pot, pi)
        for g in range(blocks // GROUP):
            rows = jnp.concatenate(
                [turned[pl.ds(64 * s + GROUP * g + q, n, stride=128), :] for q in range(GROUP)], 0
            )
            wide = jnp.where(diagonal, jnp.concatenate([rows] * GROUP, 1), 0.0)
            at_hi, at_lo = split(jnp.transpose(wide))
            at_ref[s, g, 0] = at_hi
            at_ref[s, g, 1] = at_lo
            hi, lo = split(wide)
            hi = mm(pot, mm(hi, pi).astype(BF16))
            lo = mm(pot, mm(lo, pi).astype(BF16))
            rot = 2.0 * (hi + lo) - ident
            m_ref[s, g, 0], m_ref[s, g, 1] = split(rot)
            mt_ref[s, g, 0], mt_ref[s, g, 1] = split(jnp.transpose(rot))


def rotations(skew, pi, pot):
    n = skew.shape[-1]
    groups = skew.shape[1] // GROUP
    width = GROUP * n
    shape = jax.ShapeDtypeStruct((2, groups, 2, width, width), BF16)
    return pl.pallas_call(
        rot_kernel,
        out_shape=(shape, shape, shape),
        in_specs=[VMEM] * 3,
        out_specs=(VMEM,) * 3,
        scratch_shapes=[
            pltpu.VMEM((n * n, 128), F32),
            pltpu.VMEM((n * n, 128), F32),
            pltpu.VMEM((n * 128, n), F32),
        ],
        compiler_params=PARAMS,
        cost_estimate=pl.CostEstimate(flops=10**9, bytes_accessed=4 * 10**6, transcendentals=0),
        name="rotations",
    )(jnp.transpose(skew, (0, 2, 3, 1)), pi, pot)


def pieces(a_ref, b_ref, g, half):
    span = slice(g * half, (g + 1) * half)
    return a_ref[span, :], b_ref[span, :]


def turn_kernel(scaled, a_ref, b_ref, m_ref, *rest):
    if scaled:
        sa_ref, sb_ref, oa_ref, ob_ref = rest
    else:
        oa_ref, ob_ref = rest
    groups = m_ref.shape[0]
    half = a_ref.shape[0] // groups
    for g in range(groups):
        x = jnp.concatenate(pieces(a_ref, b_ref, g, half), 0)
        hi, lo = m_ref[g, 0], m_ref[g, 1]
        if scaled == "before":
            x = x.astype(F32) * jnp.concatenate(pieces(sa_ref, sb_ref, g, half), 0)
            x, low = split(x)
            y = mm(hi, x) + (mm(lo, x) + mm(hi, low))
        else:
            y = mm(hi, x) + mm(lo, x)
        if scaled == "after":
            y = y * jnp.concatenate(pieces(sa_ref, sb_ref, g, half), 0)
        y = y.astype(BF16)
        oa_ref[g * half : (g + 1) * half, :] = y[:half]
        ob_ref[g * half : (g + 1) * half, :] = y[half:]


def turn(a, b, m, scaled=None, scales=()):
    shape = jax.ShapeDtypeStruct(a.shape, BF16)
    return pl.pallas_call(
        functools.partial(turn_kernel, scaled),
        out_shape=(shape, shape),
        in_specs=[VMEM] * (3 + len(scales)),
        out_specs=(VMEM, VMEM),
        compiler_params=PARAMS,
        cost_estimate=pl.CostEstimate(flops=2 * 10**8, bytes_accessed=3 * 10**6, transcendentals=0),
        name="turn",
    )(a, b, m, *scales)


def grad_kernel(norm, q1a, q1b, sa, sb, p1a, p1b, q0a, q0b, p0a, p0b, at_ref, po_ref, pit_ref, out_ref):
    groups = at_ref.shape[1]
    width = at_ref.shape[-1]
    n = width // GROUP
    half = q1a.shape[0] // groups
    r = lax.broadcasted_iota(jnp.int32, (width, width), 0)
    c = lax.broadcasted_iota(jnp.int32, (width, width), 1)
    same = (r % half) // (n // 2) == (c % half) // (n // 2)
    u = lax.broadcasted_iota(jnp.int32, (n, width), 0)
    v = lax.broadcasted_iota(jnp.int32, (n, width), 1) % n
    nt = (((1,), (1,)), ((), ()))
    for g in range(groups):
        dense = []
        for s in range(2):
            if s == 0:
                q = jnp.concatenate(pieces(q0a, q0b, g, half), 0)
                p = jnp.concatenate(pieces(p0a, p0b, g, half), 0)
            else:
                q = jnp.concatenate(pieces(q1a, q1b, g, half), 0).astype(F32)
                q = (q * jnp.concatenate(pieces(sa, sb, g, half), 0)).astype(BF16)
                p = jnp.concatenate(pieces(p1a, p1b, g, half), 0)
            cross = lax.dot_general(q, p, nt, preferred_element_type=F32)
            cross = jnp.where(same, cross, 0.0).astype(BF16)
            plain = mm(mm(po_ref[s], cross).astype(BF16), pit_ref[s]).astype(BF16)
            hi, lo = at_ref[s, g, 0], at_ref[s, g, 1]
            left = (mm(hi, plain) + mm(lo, plain)).astype(BF16)
            full = mm(left, hi) + mm(left, lo)
            full = (full - jnp.transpose(full)) * (-2.0 * norm)
            dense.append(full[:n] + full[n : 2 * n] + full[2 * n : 3 * n] + full[3 * n :])
        out_ref[g * n : (g + 1) * n, :] = jnp.where(u < v, dense[0], dense[1])


def hidden_kernel(at_ref, own_ref, r1, r2, r3, core_ref, w_ref, keep_ref, send_ref, x_all):
    size = own_ref.shape[1]

    @pl.when(pl.program_id(0) == 0)
    def _():
        zi, xi, ci = at_ref[0], at_ref[1], at_ref[2]
        for d in range(4):
            src = (own_ref, r1, r2, r3)[d]
            for r in range(4):
                place = ((zi ^ r) * 4 + (xi + 4 - d) % 4) * 2
                x_all[pl.ds(pl.multiple_of((place + ci) * size, 16), size), :] = src[r]
                x_all[pl.ds(pl.multiple_of((place + 1 - ci) * size, 16), size), :] = core_ref[d, r]

    y = mm(w_ref[...], x_all[...]).astype(BF16)
    upper = at_ref[0] >= 2
    blocks = y.shape[0] // 32
    y = y.reshape(blocks, 2, 16, y.shape[1])
    first, second = y[:, 0].reshape(-1, y.shape[3]), y[:, 1].reshape(-1, y.shape[3])
    keep_ref[...] = jnp.where(upper, second, first)
    send_ref[...] = jnp.where(upper, first, second)


def hidden_halves(place, own, r1, r2, r3, core, weight):
    rows, depth = weight.shape
    cols = own.shape[-1]
    steps = 4
    shape = jax.ShapeDtypeStruct((rows // 2, cols), BF16)
    out = pl.BlockSpec((rows // 2 // steps, cols), lambda i: (i, 0))
    return pl.pallas_call(
        hidden_kernel,
        grid=(steps,),
        out_shape=(shape, shape),
        in_specs=[SMEM] + [VMEM] * 5 + [pl.BlockSpec((rows // steps, depth), lambda i: (i, 0))],
        out_specs=(out, out),
        scratch_shapes=[pltpu.VMEM((depth, cols), BF16)],
        compiler_params=PARAMS,
        cost_estimate=pl.CostEstimate(
            flops=2 * rows * depth * cols, bytes_accessed=2 * rows * depth, transcendentals=0
        ),
        name="hidden",
    )(place, own, r1, r2, r3, core, weight)


def input_kernel(at_ref, own_ref, other_ref, w_ref, keep_ref, send_ref, gt):
    @pl.when(pl.program_id(0) == 0)
    def _():
        upper = at_ref[0] >= 2
        a, b = own_ref[...], other_ref[...]
        cols = a.shape[1]
        first = jnp.where(upper, b, a).reshape(-1, 1, 16, cols)
        second = jnp.where(upper, a, b).reshape(-1, 1, 16, cols)
        whole = jnp.concatenate([first, second], 1).reshape(-1, cols)
        gt[...] = jnp.transpose(whole)

    y = jnp.transpose(mm(gt[...], w_ref[...])).astype(BF16)
    size = keep_ref.shape[2]
    high = at_ref[2] == 1
    for x in range(4):
        lo = y[2 * x * size : (2 * x + 1) * size]
        hi = y[(2 * x + 1) * size : (2 * x + 2) * size]
        keep_ref[0, x] = jnp.where(high, hi, lo)
        send_ref[0, x] = jnp.where(high, lo, hi)


def input_parts(place, own, other, weight):
    rows, depth = weight.shape
    cols = own.shape[-1]
    steps = 4
    shape = jax.ShapeDtypeStruct((4, 4, depth // 32, cols), BF16)
    out = pl.BlockSpec((1, 4, depth // 32, cols), lambda i: (i, 0, 0, 0))
    return pl.pallas_call(
        input_kernel,
        grid=(steps,),
        out_shape=(shape, shape),
        in_specs=[SMEM] + [VMEM] * 2 + [pl.BlockSpec((rows, depth // steps), lambda i: (0, i))],
        out_specs=(out, out),
        scratch_shapes=[pltpu.VMEM((cols, rows), BF16)],
        compiler_params=PARAMS,
        cost_estimate=pl.CostEstimate(
            flops=2 * rows * depth * cols, bytes_accessed=2 * rows * depth, transcendentals=0
        ),
        name="input_sums",
    )(place, own, other, weight)


def halves(x, high):
    shaped = x.reshape(-1, 2, 16, x.shape[1])
    first, second = shaped[:, 0].reshape(-1, x.shape[1]), shaped[:, 1].reshape(-1, x.shape[1])
    return jnp.where(high, second, first), jnp.where(high, first, second)


def join(own, other, high):
    cols = own.shape[1]
    first = jnp.where(high, other, own).reshape(-1, 1, 16, cols)
    second = jnp.where(high, own, other).reshape(-1, 1, 16, cols)
    return jnp.concatenate([first, second], 1).reshape(-1, cols)


A_PAIRS = [(0, 0), (1, 2), (2, 1), (3, 3)]
B_PAIRS = [(0, 2), (1, 0), (2, 3), (3, 1)]
B_BACK = [(b, a) for a, b in B_PAIRS]


def per_device(responses, weight, skew, section_perm, prefix_ids, prefix_scale, out_grad):
    zi, xi, ci = lax.axis_index("z"), lax.axis_index("x"), lax.axis_index("c")
    yi = lax.axis_index("y")
    p, q = zi // 2, zi % 2
    place = jnp.stack([zi, xi, ci]).astype(jnp.int32)
    n = skew.shape[-1]
    width = GROUP * n
    mine = responses.T
    along_z = jnp.stack([mine] + [xor(mine, "z", k) for k in (1, 2, 3)])
    g_own, g_send = halves(out_grad, q == 1)
    g_rec = xor(g_send, "z", 1)
    scale_rec = xor(prefix_scale, "z", 1)
    x2 = shift(along_z, "x", 2)
    x1 = shift(along_z, "x", 1)
    x3 = shift(along_z, "x", 3)
    row = jnp.arange(width)
    slot, group_of = row // (width // 2), (row // 16) % GROUP

    def one_hot(s, bit):
        spot = (slot ^ bit) * 16 + row % 16
        target = jnp.tile(section_perm[s], GROUP)
        return (target[:, None] == spot[None, :]) & ((row // n)[:, None] == group_of[None, :])

    pi = jnp.stack([one_hot(0, p), one_hot(1, p)]).astype(BF16)
    po = jnp.stack([one_hot(0, q), one_hot(1, q)]).astype(BF16)
    pit, pot = jnp.swapaxes(pi, 1, 2), jnp.swapaxes(po, 1, 2)
    m, mt, at = rotations(skew, pi, pot)
    onehot = (prefix_ids[None, :] == jnp.arange(prefix_scale.shape[0], dtype=jnp.int32)[:, None]).astype(F32)

    def rows_of(table):
        return lax.dot_general(table, onehot, (((0,), (0,)), ((), ())), precision=lax.Precision.HIGHEST)

    s_own, _ = halves(rows_of(prefix_scale), q == 1)
    s_rec, _ = halves(rows_of(scale_rec), q == 1)
    ga, gb = turn(g_own, g_rec, mt[1], "before", (s_own, s_rec))
    ga = lax.ppermute(ga, "z", A_PAIRS)
    gb = lax.ppermute(gb, "z", B_BACK)
    by_x = jnp.stack([along_z, x1, x2, x3])
    by_core = xor(by_x, "c", 1)
    z_own, z_send = hidden_halves(place, along_z, x1, x2, x3, by_core, weight)
    z_rec = xor(z_send, "z", 2)
    h_own, h_send = turn(ga, gb, mt[0])
    h_rec = xor(h_send, "z", 2)
    za, zb = turn(z_own, z_rec, m[0])
    za = lax.ppermute(za, "z", A_PAIRS)
    zb = lax.ppermute(zb, "z", B_PAIRS)
    keep, send = input_parts(place, h_own, h_rec, weight)
    part = keep.astype(F32) + xor(send, "c", 1).astype(F32)
    part_bf = part.astype(BF16)

    def for_x(d):
        return lax.dynamic_index_in_dim(part_bf, (xi + d) % 4, 1, keepdims=False)

    total = lax.dynamic_index_in_dim(part, xi, 1, keepdims=False)
    total = total + sum(shift(for_x(d), "x", d).astype(F32) for d in (2, 1, 3))
    total_bf = total.astype(BF16)
    final = lax.dynamic_index_in_dim(total, zi, 0, keepdims=False)
    final = final + sum(
        xor(lax.dynamic_index_in_dim(total_bf, zi ^ k, 0, keepdims=False), "z", k).astype(F32)
        for k in (1, 2, 3)
    )
    input_grad = final.astype(BF16)
    j_own, j_send = turn(za, zb, m[1], "after", (s_own, s_rec))
    j_rec = xor(j_send, "z", 1)
    judged = join(j_own, j_rec, q == 1)
    rows_all = responses.shape[0] * lax.axis_size("y") * lax.axis_size("h")
    partial = pl.pallas_call(
        functools.partial(grad_kernel, 1.0 / rows_all**0.5),
        out_shape=jax.ShapeDtypeStruct((m.shape[1] * n, width), F32),
        in_specs=[VMEM] * 13,
        out_specs=VMEM,
        compiler_params=PARAMS,
        cost_estimate=pl.CostEstimate(flops=10**9, bytes_accessed=5 * 10**6, transcendentals=0),
        name="rotation_grad",
    )(g_own, g_rec, s_own, s_rec, za, zb, ga, gb, z_own, z_rec, at, po, pit)
    y0, y1 = yi % 2, yi // 2
    part4 = partial.reshape(2, 2, -1, width)
    half = lax.dynamic_index_in_dim(part4, y0, 0, keepdims=False)
    half = half + xor(lax.dynamic_index_in_dim(part4, 1 - y0, 0, keepdims=False), "y", 1)
    quarter = lax.dynamic_index_in_dim(half, y1, 0, keepdims=False)
    quarter = quarter + xor(lax.dynamic_index_in_dim(half, 1 - y1, 0, keepdims=False), "y", 2)
    quarter = quarter + xor(quarter, "h", 1)
    other = xor(quarter, "y", 2)
    half = jnp.where(y1 == 0, jnp.stack([quarter, other]), jnp.stack([other, quarter]))
    other = xor(half, "y", 1)
    summed = jnp.where(y0 == 0, jnp.stack([half, other]), jnp.stack([other, half]))
    packed = summed.reshape(-1, n, GROUP, n).transpose(1, 3, 0, 2).reshape(n, n, -1)
    u = jnp.arange(n)[:, None, None]
    v = jnp.arange(n)[None, :, None]
    upper = jnp.where(u < v, packed, 0.0)
    lower = jnp.where(u > v, packed, 0.0)
    both = jnp.stack([upper - jnp.swapaxes(upper, 0, 1), lower - jnp.swapaxes(lower, 0, 1)])
    return judged, input_grad, jnp.transpose(both, (0, 3, 1, 2))


def solution(mesh):
    wide = Mesh(mesh.devices.reshape(4, 2, 4, 4, 2), ("y", "h", "z", "x", "c"))
    dp, mp = ("y", "h"), ("z", "x", "c")
    in_specs = (
        P(dp, mp),
        P(mp, None),
        P(None, mp, None, None),
        P(),
        P(dp),
        P(None, mp),
        P(mp, dp),
    )
    out_specs = (P(mp, dp), P(mp, dp), P(None, mp, None, None))
    return jax.shard_map(per_device, mesh=wide, in_specs=in_specs, out_specs=out_specs, check_vma=False)
```

```python
import functools

import jax
import jax.numpy as jnp
from jax import lax
from jax.experimental import pallas as pl
from jax.experimental.pallas import tpu as pltpu
from jax.sharding import Mesh, PartitionSpec as P

F32 = jnp.float32
BF16 = jnp.bfloat16
GROUP = 4
VMEM_LIMIT = 12 * 1024 * 1024
WEIGHT_LIMIT = 24 * 1024 * 1024

VMEM = pl.BlockSpec(memory_space=pltpu.VMEM)
SMEM = pl.BlockSpec(memory_space=pltpu.SMEM)
ANY = pl.BlockSpec(memory_space=pl.ANY)
HBM = pl.BlockSpec(memory_space=pltpu.HBM)
PARAMS = pltpu.CompilerParams(vmem_limit_bytes=VMEM_LIMIT)
WEIGHT_PARAMS = pltpu.CompilerParams(vmem_limit_bytes=WEIGHT_LIMIT)
STEPS = 4


def cost(us):
    return pl.CostEstimate(flops=int(us * 1.15e9), bytes_accessed=0, transcendentals=0)


def xor(x, axis, k):
    return lax.ppermute(x, axis, [(i, i ^ k) for i in range(lax.axis_size(axis))])


def shift(x, axis, k):
    n = lax.axis_size(axis)
    return lax.ppermute(x, axis, [(i, (i + k) % n) for i in range(n)])


def mm(a, b):
    return jnp.dot(a, b, preferred_element_type=F32)


def split(x):
    hi = x.astype(BF16)
    return hi, (x - hi.astype(F32)).astype(BF16)


def fill_kernel(k_ref, dep_ref, mat, raw):
    n = k_ref.shape[1]
    blocks = k_ref.shape[3]
    raw[...] = jnp.zeros_like(raw)
    for s in range(2):
        raw[:, 64 * s : 64 * s + blocks] = k_ref[s].reshape(n * n, blocks)
    sub = lax.broadcasted_iota(jnp.int32, (n, 128), 0)
    for u in range(n):
        mat[u * n : (u + 1) * n, :] = (
            raw[u * n : (u + 1) * n, :] - raw[pl.ds(u, n, stride=n), :]
            + jnp.where(sub == u, 1.0, 0.0)
        )

    def eliminate(k, carry):
        at = sub == k
        base = pl.multiple_of(k * n, n)
        pivot = 1.0 / mat[pl.ds(base + k, 1), :]
        row = jnp.where(at, 1.0, mat[pl.ds(base, n), :]) * pivot
        for i in range(n):
            factor = mat[pl.ds(i * n + k, 1), :]
            mine = jnp.where(at, 0.0, mat[i * n : (i + 1) * n, :])
            mat[i * n : (i + 1) * n, :] = mine - factor * row
        mat[pl.ds(base, n), :] = row
        return carry

    lax.fori_loop(0, n, eliminate, 0)


def one_hots(at_ref, perm_ref, s, n):
    width = GROUP * n
    r = lax.broadcasted_iota(jnp.int32, (width, width), 0)
    c = lax.broadcasted_iota(jnp.int32, (width, width), 1)
    half = width // 2
    by_row, by_col = jnp.zeros_like(r), jnp.zeros_like(c)
    for u in range(n):
        by_row = jnp.where(r % n == u, perm_ref[s, u], by_row)
        by_col = jnp.where(c % n == u, perm_ref[s, u], by_col)

    def one_hot(raw_at, target, cut_at, bit):
        spot = ((cut_at // half) ^ bit) * 16 + cut_at % 16
        hit = (target == spot) & (raw_at // n == (cut_at // 16) % GROUP)
        return jnp.where(hit, 1.0, 0.0).astype(BF16)

    pi = one_hot(r, by_row, c, at_ref[0] // 2)
    pot = one_hot(c, by_col, r, at_ref[0] % 2)
    return pi, pot, r // n == c // n


def wide_block(turned, s, g, groups, n, diagonal):
    rows = [turned[pl.ds(64 * s + g + groups * q, n, stride=128), :] for q in range(GROUP)]
    return jnp.where(diagonal, jnp.concatenate([jnp.concatenate(rows, 0)] * GROUP, 1), 0.0)


def invert_kernel(at_ref, perm_ref, k_ref, dep_ref, turned, mt_ref, mat, raw):
    fill_kernel(k_ref, dep_ref, mat, raw)
    n = k_ref.shape[1]
    groups = mt_ref.shape[0]
    for u in range(n):
        turned[u * 128 : (u + 1) * 128, :] = jnp.transpose(mat[u * n : (u + 1) * n, :])
    pi, pot, diagonal = one_hots(at_ref, perm_ref, 1, n)
    ident = mm(pot, pi)
    for g in range(groups):
        hi, lo = split(wide_block(turned, 1, g, groups, n, diagonal))
        rot = mm(pot, mm(hi, pi).astype(BF16)) + mm(pot, mm(lo, pi).astype(BF16))
        mt_ref[g, 0], mt_ref[g, 1] = split(jnp.transpose(2.0 * rot - ident))


def build_kernel(at_ref, perm_ref, turned, dep_ref, m0_ref, mt0_ref, m1_ref, l_ref, r_ref):
    groups = l_ref.shape[1]
    n = l_ref.shape[-1] // GROUP
    for s in range(2):
        pi, pot, diagonal = one_hots(at_ref, perm_ref, s, n)
        ident = mm(pot, pi)
        for g in range(groups):
            hi, lo = split(wide_block(turned, s, g, groups, n, diagonal))
            right_hi, right_lo = mm(hi, pi), mm(lo, pi)
            left = mm(pot, hi) + mm(pot, lo)
            l_ref[s, g, 0], l_ref[s, g, 1] = split(jnp.transpose(left))
            r_ref[s, g, 0], r_ref[s, g, 1] = split(jnp.transpose(right_hi + right_lo))
            rot = mm(pot, right_hi.astype(BF16)) + mm(pot, right_lo.astype(BF16))
            rot = 2.0 * rot - ident
            m_ref = m1_ref if s else m0_ref
            m_ref[g, 0], m_ref[g, 1] = split(rot)
            if s == 0:
                mt0_ref[g, 0], mt0_ref[g, 1] = split(jnp.transpose(rot))


def invert(place, section_perm, skew, after):
    n = skew.shape[-1]
    groups = skew.shape[1] // GROUP
    width = GROUP * n
    return pl.pallas_call(
        invert_kernel,
        out_shape=(
            jax.ShapeDtypeStruct((n * 128, n), F32),
            jax.ShapeDtypeStruct((groups, 2, width, width), BF16),
        ),
        in_specs=[SMEM] * 2 + [VMEM, ANY],
        out_specs=(VMEM, VMEM),
        scratch_shapes=[pltpu.VMEM((n * n, 128), F32), pltpu.VMEM((n * n, 128), F32)],
        compiler_params=PARAMS,
        cost_estimate=cost(7),
        name="invert",
    )(place, section_perm, jnp.transpose(skew, (0, 2, 3, 1)), after)


def build(place, section_perm, turned, after):
    n = turned.shape[1]
    groups = after.shape[0] // (16 * GROUP)
    width = GROUP * n
    one = jax.ShapeDtypeStruct((groups, 2, width, width), BF16)
    two = jax.ShapeDtypeStruct((2, groups, 2, width, width), BF16)
    return pl.pallas_call(
        build_kernel,
        out_shape=(one, one, one, two, two),
        in_specs=[SMEM] * 2 + [VMEM, ANY],
        out_specs=(VMEM,) * 5,
        compiler_params=PARAMS,
        cost_estimate=cost(5),
        name="build",
    )(place, section_perm, turned, after)


def spans(g, groups):
    return [slice(16 * (g + groups * q), 16 * (g + groups * q + 1)) for q in range(GROUP)]


def both(a_ref, b_ref, g, groups):
    rows = spans(g, groups)
    return jnp.concatenate([a_ref[row, :] for row in rows] + [b_ref[row, :] for row in rows], 0)


def put(oa_ref, ob_ref, g, groups, y):
    half = y.shape[0] // 2
    for q, row in enumerate(spans(g, groups)):
        oa_ref[row, :] = y[16 * q : 16 * (q + 1)]
        ob_ref[row, :] = y[half + 16 * q : half + 16 * (q + 1)]


def turn_kernel(a_ref, b_ref, m_ref, *rest):
    oa_ref, ob_ref = rest[-2:]
    groups = m_ref.shape[0]
    for g in range(groups):
        x = both(a_ref, b_ref, g, groups)
        y = mm(m_ref[g, 0], x) + mm(m_ref[g, 1], x)
        put(oa_ref, ob_ref, g, groups, y.astype(BF16))


def turn(a, b, m, after):
    shape = jax.ShapeDtypeStruct(a.shape, BF16)
    return pl.pallas_call(
        turn_kernel,
        out_shape=(shape, shape),
        in_specs=[VMEM] * 3 + [ANY] * len(after),
        out_specs=(VMEM, VMEM),
        compiler_params=PARAMS,
        cost_estimate=cost(1),
        name="turn",
    )(a, b, m, *after)


def scale_rows(ps_ref, ids, high):
    table = jnp.transpose(ps_ref[...])
    parts = []
    for _ in range(3):
        hi, _rest = split(table)
        parts.append(hi)
        table = table - hi.astype(F32)
    wanted = lax.broadcasted_iota(jnp.int32, (3 * ps_ref.shape[0], ids.shape[1]), 0) % ps_ref.shape[0]
    onehot = jnp.where(ids == wanted, 1.0, 0.0).astype(BF16)
    whole = mm(jnp.concatenate(parts, 1), onehot).reshape(-1, 2, 16, ids.shape[1])
    return jnp.where(high, whole[:, 1], whole[:, 0]).reshape(-1, ids.shape[1])


def scaled_cotangent(high, grad_ref, rec_ref, sa_ref, sb_ref, g, groups):
    rows = spans(g, groups)
    own = [grad_ref[2 * row.start : 2 * row.stop, :].reshape(2, 16, -1) for row in rows]
    own = [jnp.where(high, x[1], x[0]) for x in own]
    x = jnp.concatenate(own + [rec_ref[row, :] for row in rows], 0).astype(F32)
    return x * both(sa_ref, sb_ref, g, groups)


def cotangent_kernel(at_ref, grad_ref, rec_ref, mine_ref, theirs_ref, ids_ref, mt_ref, *rest):
    oa_ref, ob_ref, sa_ref, sb_ref = rest
    high = at_ref[0] % 2 == 1
    ids = ids_ref[...]
    sa_ref[...] = scale_rows(mine_ref, ids, high)
    sb_ref[...] = scale_rows(theirs_ref, ids, high)
    groups = mt_ref.shape[0]
    for g in range(groups):
        hi, lo = split(scaled_cotangent(high, grad_ref, rec_ref, sa_ref, sb_ref, g, groups))
        y = mm(mt_ref[g, 0], hi) + (mm(mt_ref[g, 1], hi) + mm(mt_ref[g, 0], lo))
        put(oa_ref, ob_ref, g, groups, y.astype(BF16))


def cotangent(place, out_grad, rec, mine, theirs, ids, mt):
    shape = jax.ShapeDtypeStruct(rec.shape, BF16)
    return pl.pallas_call(
        cotangent_kernel,
        out_shape=(shape, shape),
        in_specs=[SMEM] + [VMEM] * 6,
        out_specs=(VMEM, VMEM),
        scratch_shapes=[pltpu.VMEM(rec.shape, F32)] * 2,
        compiler_params=PARAMS,
        cost_estimate=cost(3),
        name="cotangent",
    )(place, out_grad, rec, mine, theirs, ids, mt)


def last_kernel(norm, at_ref, y0_ref, grad_ref, rec_ref, mine_ref, theirs_ref, ids_ref, *rest):
    (m_ref, p1a, p1b, q0a, q0b, p0a, p0b, l_ref, r_ref, dep_ref) = rest[:10]
    (ja_ref, jb_ref, keep_ref, send_ref, hold, out_ref, sa_ref, sb_ref) = rest[10:]
    high = at_ref[0] % 2 == 1
    ids = ids_ref[...]
    sa_ref[...] = scale_rows(mine_ref, ids, high)
    sb_ref[...] = scale_rows(theirs_ref, ids, high)
    groups = l_ref.shape[1]
    width = l_ref.shape[-1]
    n = width // GROUP
    r = lax.broadcasted_iota(jnp.int32, (width, width), 0)
    c = lax.broadcasted_iota(jnp.int32, (width, width), 1)
    same = (r // 16) % GROUP == (c // 16) % GROUP
    u = lax.broadcasted_iota(jnp.int32, (n, width), 0)
    v = lax.broadcasted_iota(jnp.int32, (n, width), 1) % n
    nt = (((1,), (1,)), ((), ()))
    every = [(s, g) for s in range(2) for g in range(groups)]
    for s, g in every:
        if s == 0:
            q = both(q0a, q0b, g, groups)
            p = both(p0a, p0b, g, groups)
        else:
            q = scaled_cotangent(high, grad_ref, rec_ref, sa_ref, sb_ref, g, groups).astype(BF16)
            p = both(p1a, p1b, g, groups)
            y = (mm(m_ref[g, 0], p) + mm(m_ref[g, 1], p)) * both(sa_ref, sb_ref, g, groups)
            put(ja_ref, jb_ref, g, groups, y.astype(BF16))
        cross = lax.dot_general(q, p, nt, preferred_element_type=F32)
        hold[s, g] = jnp.where(same, cross, 0.0).astype(BF16)
    for s, g in every:
        x = hold[s, g]
        hold[s, g] = (mm(l_ref[s, g, 0], x) + mm(l_ref[s, g, 1], x)).astype(BF16)
    for g in range(groups):
        dense = []
        for s in range(2):
            x = hold[s, g]
            full = mm(x, r_ref[s, g, 0]) + mm(x, r_ref[s, g, 1])
            full = (full - jnp.transpose(full)) * (-2.0 * norm)
            dense.append(full[:n] + full[n : 2 * n] + full[2 * n : 3 * n] + full[3 * n :])
        out_ref[g * n : (g + 1) * n, :] = jnp.where(u < v, dense[0], dense[1])
    size = keep_ref.shape[0]
    y0 = y0_ref[0]
    keep_ref[...] = out_ref[pl.ds(pl.multiple_of(y0 * size, 8), size), :]
    send_ref[...] = out_ref[pl.ds(pl.multiple_of((1 - y0) * size, 8), size), :]


def unpack_kernel(y0_ref, mine_ref, other_ref, out_ref, packed, planes):
    size = mine_ref.shape[0]
    y0 = y0_ref[0]
    packed[pl.ds(pl.multiple_of(y0 * size, 8), size), :] = mine_ref[...]
    packed[pl.ds(pl.multiple_of((1 - y0) * size, 8), size), :] = other_ref[...]
    n = out_ref.shape[1]
    groups = packed.shape[0] // n
    for u in range(n):
        x = jnp.transpose(packed[pl.ds(u, groups, stride=n), :])
        planes[u * n : (u + 1) * n, :] = jnp.concatenate([x[q * n : (q + 1) * n] for q in range(GROUP)], 1)
    v = lax.broadcasted_iota(jnp.int32, (n, planes.shape[1]), 0)
    for u in range(n):
        x = planes[u * n : (u + 1) * n, :]
        y = planes[pl.ds(u, n, stride=n), :]
        out_ref[0, u] = jnp.where(v > u, x, 0.0) - jnp.where(v < u, y, 0.0)
        out_ref[1, u] = jnp.where(v < u, x, 0.0) - jnp.where(v > u, y, 0.0)


def gather_kernel(a_ref, b_ref, c_ref, d_ref, dep_ref, out_ref):
    for i, ref in enumerate((a_ref, b_ref, c_ref, d_ref)):
        out_ref[i] = ref[...]


def hidden_kernel(at_ref, own_ref, r1, r2, r3, core_ref, w_ref, keep_ref, send_ref, x_all):
    size = own_ref.shape[1]
    rows = w_ref.shape[0] // STEPS
    zi, xi, ci = at_ref[0], at_ref[1], at_ref[2]
    for d in range(4):
        src = (own_ref, r1, r2, r3)[d]
        for r in range(4):
            place = ((zi ^ r) * 4 + (xi + 4 - d) % 4) * 2
            x_all[pl.ds(pl.multiple_of((place + ci) * size, 16), size), :] = src[r]
            x_all[pl.ds(pl.multiple_of((place + 1 - ci) * size, 16), size), :] = core_ref[d, r]
    upper = zi >= 2
    for i in range(STEPS):
        y = mm(w_ref[i * rows : (i + 1) * rows, :], x_all[...]).astype(BF16)
        y = y.reshape(-1, 2, 16, y.shape[1])
        first, second = y[:, 0].reshape(-1, y.shape[3]), y[:, 1].reshape(-1, y.shape[3])
        span = slice(i * (rows // 2), (i + 1) * (rows // 2))
        keep_ref[span, :] = jnp.where(upper, second, first)
        send_ref[span, :] = jnp.where(upper, first, second)


def hidden_halves(place, own, r1, r2, r3, core, weight):
    rows, depth = weight.shape
    cols = own.shape[-1]
    shape = jax.ShapeDtypeStruct((rows // 2, cols), BF16)
    return pl.pallas_call(
        hidden_kernel,
        out_shape=(shape, shape),
        in_specs=[SMEM] + [VMEM] * 6,
        out_specs=(VMEM, VMEM),
        scratch_shapes=[
            pltpu.VMEM((depth, cols), BF16),
        ],
        compiler_params=WEIGHT_PARAMS,
        cost_estimate=cost(6),
        name="hidden",
    )(place, own, r1, r2, r3, core, weight)


def input_kernel(at_ref, own_ref, other_ref, w_ref, dep_ref, keep_ref, send_ref, gt, y_all):
    depth = w_ref.shape[1] // STEPS
    zi, xi, ci = at_ref[0], at_ref[1], at_ref[2]
    upper = zi >= 2
    a, b = own_ref[...], other_ref[...]
    cols = a.shape[1]
    first = jnp.where(upper, b, a).reshape(-1, 1, 16, cols)
    second = jnp.where(upper, a, b).reshape(-1, 1, 16, cols)
    whole = jnp.concatenate([first, second], 1).reshape(-1, cols)
    gt[...] = jnp.transpose(whole)
    size = keep_ref.shape[2]
    for z in range(STEPS):
        y_all[...] = jnp.transpose(mm(gt[...], w_ref[:, z * depth : (z + 1) * depth]))
        for d in range(4):
            spot = ((xi + d) % 4) * 2
            keep_ref[d, z ^ zi] = y_all[pl.ds(pl.multiple_of((spot + ci) * size, 16), size), :]
            send_ref[d, z ^ zi] = y_all[pl.ds(pl.multiple_of((spot + 1 - ci) * size, 16), size), :].astype(BF16)


def input_parts(place, own, other, weight, after):
    rows, depth = weight.shape
    cols = own.shape[-1]
    dims = (4, 4, depth // 32, cols)
    return pl.pallas_call(
        input_kernel,
        out_shape=(jax.ShapeDtypeStruct(dims, F32), jax.ShapeDtypeStruct(dims, BF16)),
        in_specs=[SMEM] + [VMEM] * 3 + [ANY],
        out_specs=(VMEM, VMEM),
        scratch_shapes=[
            pltpu.VMEM((cols, rows), BF16),
            pltpu.VMEM((depth // STEPS, cols), F32),
        ],
        compiler_params=WEIGHT_PARAMS,
        cost_estimate=cost(6),
        name="input_sums",
    )(place, own, other, weight, after)


def join_kernel(at_ref, own_ref, other_ref, out_ref):
    high = at_ref[0] % 2 == 1
    a, b = own_ref[...], other_ref[...]
    cols = a.shape[1]
    first = jnp.where(high, b, a).reshape(-1, 1, 16, cols)
    second = jnp.where(high, a, b).reshape(-1, 1, 16, cols)
    out_ref[...] = jnp.concatenate([first, second], 1).reshape(-1, cols)


A_PAIRS = [(0, 0), (1, 2), (2, 1), (3, 3)]
B_PAIRS = [(0, 2), (1, 0), (2, 3), (3, 1)]
B_BACK = [(b, a) for a, b in B_PAIRS]


def per_device(responses, weight, skew, section_perm, prefix_ids, prefix_scale, out_grad):
    zi, xi, ci = lax.axis_index("z"), lax.axis_index("x"), lax.axis_index("c")
    yi = lax.axis_index("y")
    q = lax.bitwise_and(zi, 1)
    place = jnp.stack([zi, xi, ci]).astype(jnp.int32)
    n = skew.shape[-1]
    width = GROUP * n
    cols = responses.shape[0]
    mine = responses.T
    along_z = jnp.stack([mine] + [xor(mine, "z", k) for k in (1, 2, 3)])
    g_send = lax.dynamic_index_in_dim(out_grad.reshape(-1, 2, 16, cols), 1 - q, 1, keepdims=False)
    g_rec = xor(g_send.reshape(-1, cols), "z", 1)
    scale_rec = xor(prefix_scale, "z", 1)
    x2 = shift(along_z, "x", 2)
    x1 = shift(along_z, "x", 1)
    x3 = shift(along_z, "x", 3)
    turned, mt1 = invert(place, section_perm, skew, along_z)
    ids = prefix_ids[None, :]
    ga_out, gb_out = cotangent(place, out_grad, g_rec, prefix_scale, scale_rec, ids, mt1)
    ga = lax.ppermute(ga_out, "z", A_PAIRS)
    gb = lax.ppermute(gb_out, "z", B_BACK)
    by_x = pl.pallas_call(
        gather_kernel,
        out_shape=jax.ShapeDtypeStruct((4,) + along_z.shape, BF16),
        in_specs=[VMEM] * 4 + [ANY],
        out_specs=VMEM,
        compiler_params=PARAMS,
        cost_estimate=cost(1),
        name="gather",
    )(along_z, x1, x2, x3, ga_out)
    by_core = xor(by_x, "c", 1)
    m0, mt0, m1, left, right = build(place, section_perm, turned, ga_out)
    z_own, z_send = hidden_halves(place, along_z, x1, x2, x3, by_core, weight)
    z_rec = xor(z_send, "z", 2)
    h_own, h_send = turn(ga, gb, mt0, (z_send,))
    h_rec = xor(h_send, "z", 2)
    za_out, zb = turn(z_own, z_rec, m0, (h_send,))
    za = lax.ppermute(za_out, "z", A_PAIRS)
    zb = lax.ppermute(zb, "z", B_PAIRS)
    keep, send = input_parts(place, h_own, h_rec, weight, za_out)
    part = keep + xor(send, "c", 1).astype(F32)
    total = part[0] + sum(shift(part[d].astype(BF16), "x", d).astype(F32) for d in (2, 1, 3))
    final = total[0] + sum(xor(total[k].astype(BF16), "z", k).astype(F32) for k in (1, 2, 3))
    input_grad = final.astype(BF16)
    rows_all = cols * lax.axis_size("y") * lax.axis_size("h")
    groups = left.shape[1]
    y0 = lax.bitwise_and(yi, 1).reshape(1)
    part_of = jax.ShapeDtypeStruct((groups * n // 2, width), F32)
    half_of = jax.ShapeDtypeStruct(za.shape, BF16)
    j_own, j_send, half, half_send = pl.pallas_call(
        functools.partial(last_kernel, 1.0 / rows_all**0.5),
        out_shape=(half_of, half_of, part_of, part_of),
        in_specs=[SMEM] * 2 + [VMEM] * 14 + [ANY],
        out_specs=(VMEM,) * 4,
        scratch_shapes=[
            pltpu.VMEM((2, groups, width, width), BF16),
            pltpu.VMEM((groups * n, width), F32),
            pltpu.VMEM(za.shape, F32),
            pltpu.VMEM(za.shape, F32),
        ],
        compiler_params=PARAMS,
        cost_estimate=cost(4),
        name="last",
    )(
        place, y0, out_grad, g_rec, prefix_scale, scale_rec, ids,
        m1, za, zb, ga, gb, z_own, z_rec, left, right, send,
    )
    j_rec = xor(j_send, "z", 1)
    judged = pl.pallas_call(
        join_kernel,
        out_shape=jax.ShapeDtypeStruct(out_grad.shape, BF16),
        in_specs=[SMEM] + [VMEM] * 2,
        out_specs=VMEM,
        compiler_params=PARAMS,
        name="join",
    )(place, j_own, j_rec)
    half = half + xor(half_send, "y", 1)
    half = half + xor(half, "y", 2)
    half = half + xor(half, "h", 1)
    other = xor(half, "y", 1)
    skew_grad = pl.pallas_call(
        unpack_kernel,
        out_shape=jax.ShapeDtypeStruct((2, n, n, GROUP * groups), F32),
        in_specs=[SMEM] + [VMEM] * 2,
        out_specs=VMEM,
        scratch_shapes=[
            pltpu.VMEM((groups * n, width), F32),
            pltpu.VMEM((n * n, GROUP * groups), F32),
        ],
        compiler_params=PARAMS,
        cost_estimate=cost(2),
        name="unpack",
    )(y0, half, other)
    return judged, input_grad, jnp.transpose(skew_grad, (0, 3, 1, 2))


def solution(mesh):
    wide = Mesh(mesh.devices.reshape(4, 2, 4, 4, 2), ("y", "h", "z", "x", "c"))
    dp, mp = ("y", "h"), ("z", "x", "c")
    in_specs = (
        P(dp, mp),
        P(mp, None),
        P(None, mp, None, None),
        P(),
        P(dp),
        P(None, mp),
        P(mp, dp),
    )
    out_specs = (P(mp, dp), P(mp, dp), P(None, mp, None, None))
    return jax.shard_map(per_device, mesh=wide, in_specs=in_specs, out_specs=out_specs, check_vma=False)
```

```python
import functools

import jax
import jax.numpy as jnp
from jax import lax
from jax.experimental import pallas as pl
from jax.experimental.pallas import tpu as pltpu
from jax.sharding import Mesh, PartitionSpec as P

F32 = jnp.float32
BF16 = jnp.bfloat16
GROUP = 4
VMEM_LIMIT = 12 * 1024 * 1024
WEIGHT_LIMIT = 20 * 1024 * 1024

VMEM = pl.BlockSpec(memory_space=pltpu.VMEM)
SMEM = pl.BlockSpec(memory_space=pltpu.SMEM)
ANY = pl.BlockSpec(memory_space=pl.ANY)
HBM = pl.BlockSpec(memory_space=pltpu.HBM)
PARAMS = pltpu.CompilerParams(vmem_limit_bytes=VMEM_LIMIT)
WEIGHT_PARAMS = pltpu.CompilerParams(vmem_limit_bytes=WEIGHT_LIMIT)
STEPS = 4


def cost(us):
    return pl.CostEstimate(flops=int(us * 1.15e9), bytes_accessed=0, transcendentals=0)


def xor(x, axis, k):
    return lax.ppermute(x, axis, [(i, i ^ k) for i in range(lax.axis_size(axis))])


def shift(x, axis, k):
    n = lax.axis_size(axis)
    return lax.ppermute(x, axis, [(i, (i + k) % n) for i in range(n)])


def mm(a, b):
    return jnp.dot(a, b, preferred_element_type=F32)


def split(x):
    hi = x.astype(BF16)
    return hi, (x - hi.astype(F32)).astype(BF16)


def eliminated(k_ref, mat, raw):
    n = k_ref.shape[1]
    blocks = k_ref.shape[3]
    raw[...] = jnp.zeros_like(raw)
    for s in range(2):
        raw[:, 64 * s : 64 * s + blocks] = k_ref[s].reshape(n * n, blocks)
    sub = lax.broadcasted_iota(jnp.int32, (n, 128), 0)
    for u in range(n):
        mat[u * n : (u + 1) * n, :] = (
            raw[u * n : (u + 1) * n, :] - raw[pl.ds(u, n, stride=n), :]
            + jnp.where(sub == u, 1.0, 0.0)
        )

    def eliminate(k, carry):
        at = sub == k
        base = pl.multiple_of(k * n, n)
        pivot = 1.0 / mat[pl.ds(base + k, 1), :]
        row = jnp.where(at, 1.0, mat[pl.ds(base, n), :]) * pivot
        for i in range(n):
            factor = mat[pl.ds(i * n + k, 1), :]
            mine = jnp.where(at, 0.0, mat[i * n : (i + 1) * n, :])
            mat[i * n : (i + 1) * n, :] = mine - factor * row
        mat[pl.ds(base, n), :] = row
        return carry

    lax.fori_loop(0, n, eliminate, 0)


def one_hots(at_ref, perm_ref, s, n):
    width = GROUP * n
    r = lax.broadcasted_iota(jnp.int32, (width, width), 0)
    c = lax.broadcasted_iota(jnp.int32, (width, width), 1)
    half = width // 2
    by_row, by_col = jnp.zeros_like(r), jnp.zeros_like(c)
    for u in range(n):
        by_row = jnp.where(r % n == u, perm_ref[s, u], by_row)
        by_col = jnp.where(c % n == u, perm_ref[s, u], by_col)

    def one_hot(raw_at, target, cut_at, bit):
        spot = ((cut_at // half) ^ bit) * 16 + cut_at % 16
        hit = (target == spot) & (raw_at // n == (cut_at // 16) % GROUP)
        return jnp.where(hit, 1.0, 0.0).astype(BF16)

    pi = one_hot(r, by_row, c, at_ref[0] // 2)
    pot = one_hot(c, by_col, r, at_ref[0] % 2)
    return pi, pot, r // n == c // n


def wide_block(turned, s, g, groups, n, diagonal):
    rows = [turned[pl.ds(64 * s + g + groups * q, n, stride=128), :] for q in range(GROUP)]
    return jnp.where(diagonal, jnp.concatenate([jnp.concatenate(rows, 0)] * GROUP, 1), 0.0)


def invert_kernel(at_ref, perm_ref, k_ref, *rest):
    turned, mt_ref, mat, raw = rest[-4:]
    eliminated(k_ref, mat, raw)
    n = k_ref.shape[1]
    groups = mt_ref.shape[0]
    for u in range(n):
        turned[u * 128 : (u + 1) * 128, :] = jnp.transpose(mat[u * n : (u + 1) * n, :])
    pi, pot, diagonal = one_hots(at_ref, perm_ref, 1, n)
    ident = mm(pot, pi)
    for g in range(groups):
        hi, lo = split(wide_block(turned, 1, g, groups, n, diagonal))
        rot = mm(pot, mm(hi, pi).astype(BF16)) + mm(pot, mm(lo, pi).astype(BF16))
        mt_ref[g, 0], mt_ref[g, 1] = split(jnp.transpose(2.0 * rot - ident))


def build_kernel(at_ref, perm_ref, turned, dep_ref, m0_ref, mt0_ref, m1_ref, l_ref, r_ref):
    groups = l_ref.shape[1]
    n = l_ref.shape[-1] // GROUP
    for s in range(2):
        pi, pot, diagonal = one_hots(at_ref, perm_ref, s, n)
        ident = mm(pot, pi)
        for g in range(groups):
            hi, lo = split(wide_block(turned, s, g, groups, n, diagonal))
            right_hi, right_lo = mm(hi, pi), mm(lo, pi)
            left = mm(pot, hi) + mm(pot, lo)
            l_ref[s, g, 0], l_ref[s, g, 1] = split(jnp.transpose(left))
            r_ref[s, g, 0], r_ref[s, g, 1] = split(jnp.transpose(right_hi + right_lo))
            rot = mm(pot, right_hi.astype(BF16)) + mm(pot, right_lo.astype(BF16))
            rot = 2.0 * rot - ident
            m_ref = m1_ref if s else m0_ref
            m_ref[g, 0], m_ref[g, 1] = split(rot)
            if s == 0:
                mt0_ref[g, 0], mt0_ref[g, 1] = split(jnp.transpose(rot))


def invert(place, section_perm, skew, after):
    n = skew.shape[-1]
    groups = skew.shape[1] // GROUP
    width = GROUP * n
    return pl.pallas_call(
        invert_kernel,
        out_shape=(
            jax.ShapeDtypeStruct((n * 128, n), F32),
            jax.ShapeDtypeStruct((groups, 2, width, width), BF16),
        ),
        in_specs=[SMEM] * 2 + [VMEM] + [ANY] * len(after),
        out_specs=(VMEM, VMEM),
        scratch_shapes=[pltpu.VMEM((n * n, 128), F32), pltpu.VMEM((n * n, 128), F32)],
        compiler_params=PARAMS,
        cost_estimate=cost(7),
        name="invert",
    )(place, section_perm, jnp.transpose(skew, (0, 2, 3, 1)), *after)


def build(place, section_perm, turned, after):
    n = turned.shape[1]
    groups = after.shape[0] // (16 * GROUP)
    width = GROUP * n
    one = jax.ShapeDtypeStruct((groups, 2, width, width), BF16)
    two = jax.ShapeDtypeStruct((2, groups, 2, width, width), BF16)
    return pl.pallas_call(
        build_kernel,
        out_shape=(one, one, one, two, two),
        in_specs=[SMEM] * 2 + [VMEM, ANY],
        out_specs=(VMEM,) * 5,
        compiler_params=PARAMS,
        cost_estimate=cost(5),
        name="build",
    )(place, section_perm, turned, after)


def spans(g, groups):
    return [slice(16 * (g + groups * q), 16 * (g + groups * q + 1)) for q in range(GROUP)]


def both(a_ref, b_ref, g, groups):
    rows = spans(g, groups)
    return jnp.concatenate([a_ref[row, :] for row in rows] + [b_ref[row, :] for row in rows], 0)


def put(oa_ref, ob_ref, g, groups, y):
    half = y.shape[0] // 2
    for q, row in enumerate(spans(g, groups)):
        oa_ref[row, :] = y[16 * q : 16 * (q + 1)]
        ob_ref[row, :] = y[half + 16 * q : half + 16 * (q + 1)]


def turn_kernel(a_ref, b_ref, m_ref, *rest):
    oa_ref, ob_ref = rest[-2:]
    groups = m_ref.shape[0]
    for g in range(groups):
        x = both(a_ref, b_ref, g, groups)
        y = mm(m_ref[g, 0], x) + mm(m_ref[g, 1], x)
        put(oa_ref, ob_ref, g, groups, y.astype(BF16))


def turn(a, b, m, after):
    shape = jax.ShapeDtypeStruct(a.shape, BF16)
    return pl.pallas_call(
        turn_kernel,
        out_shape=(shape, shape),
        in_specs=[VMEM] * 3 + [ANY] * len(after),
        out_specs=(VMEM, VMEM),
        compiler_params=PARAMS,
        cost_estimate=cost(1),
        name="turn",
    )(a, b, m, *after)


def scale_rows(ps_ref, ids, high):
    table = jnp.transpose(ps_ref[...])
    parts = []
    for _ in range(3):
        hi, _rest = split(table)
        parts.append(hi)
        table = table - hi.astype(F32)
    wanted = lax.broadcasted_iota(jnp.int32, (3 * ps_ref.shape[0], ids.shape[1]), 0) % ps_ref.shape[0]
    onehot = jnp.where(ids == wanted, 1.0, 0.0).astype(BF16)
    whole = mm(jnp.concatenate(parts, 1), onehot).reshape(-1, 2, 16, ids.shape[1])
    return jnp.where(high, whole[:, 1], whole[:, 0]).reshape(-1, ids.shape[1])


def scaled_cotangent(high, grad_ref, rec_ref, sa_ref, sb_ref, g, groups):
    rows = spans(g, groups)
    own = [grad_ref[2 * row.start : 2 * row.stop, :].reshape(2, 16, -1) for row in rows]
    own = [jnp.where(high, x[1], x[0]) for x in own]
    x = jnp.concatenate(own + [rec_ref[row, :] for row in rows], 0).astype(F32)
    return x * both(sa_ref, sb_ref, g, groups)


def cotangent_kernel(at_ref, grad_ref, rec_ref, mine_ref, theirs_ref, ids_ref, mt_ref, *rest):
    oa_ref, ob_ref, sa_ref, sb_ref = rest[1:]
    high = at_ref[0] % 2 == 1
    ids = ids_ref[...]
    sa_ref[...] = scale_rows(mine_ref, ids, high)
    sb_ref[...] = scale_rows(theirs_ref, ids, high)
    groups = mt_ref.shape[0]
    for g in range(groups):
        hi, lo = split(scaled_cotangent(high, grad_ref, rec_ref, sa_ref, sb_ref, g, groups))
        y = mm(mt_ref[g, 0], hi) + (mm(mt_ref[g, 1], hi) + mm(mt_ref[g, 0], lo))
        put(oa_ref, ob_ref, g, groups, y.astype(BF16))


def cotangent(place, out_grad, rec, mine, theirs, ids, mt, after):
    shape = jax.ShapeDtypeStruct(rec.shape, BF16)
    return pl.pallas_call(
        cotangent_kernel,
        out_shape=(shape, shape),
        in_specs=[SMEM] + [VMEM] * 6 + [ANY],
        out_specs=(VMEM, VMEM),
        scratch_shapes=[pltpu.VMEM(rec.shape, F32)] * 2,
        compiler_params=PARAMS,
        cost_estimate=cost(3),
        name="cotangent",
    )(place, out_grad, rec, mine, theirs, ids, mt, after)


def last_kernel(norm, at_ref, y0_ref, grad_ref, rec_ref, mine_ref, theirs_ref, ids_ref, *rest):
    (m_ref, p1a, p1b, q0a, q0b, p0a, p0b, l_ref, r_ref, dep_ref) = rest[:10]
    (ja_ref, jb_ref, keep_ref, send_ref, hold, out_ref, sa_ref, sb_ref) = rest[10:]
    high = at_ref[0] % 2 == 1
    ids = ids_ref[...]
    sa_ref[...] = scale_rows(mine_ref, ids, high)
    sb_ref[...] = scale_rows(theirs_ref, ids, high)
    groups = l_ref.shape[1]
    width = l_ref.shape[-1]
    n = width // GROUP
    r = lax.broadcasted_iota(jnp.int32, (width, width), 0)
    c = lax.broadcasted_iota(jnp.int32, (width, width), 1)
    same = (r // 16) % GROUP == (c // 16) % GROUP
    u = lax.broadcasted_iota(jnp.int32, (n, width), 0)
    v = lax.broadcasted_iota(jnp.int32, (n, width), 1) % n
    nt = (((1,), (1,)), ((), ()))
    every = [(s, g) for s in range(2) for g in range(groups)]
    for s, g in every:
        if s == 0:
            q = both(q0a, q0b, g, groups)
            p = both(p0a, p0b, g, groups)
        else:
            q = scaled_cotangent(high, grad_ref, rec_ref, sa_ref, sb_ref, g, groups).astype(BF16)
            p = both(p1a, p1b, g, groups)
            y = (mm(m_ref[g, 0], p) + mm(m_ref[g, 1], p)) * both(sa_ref, sb_ref, g, groups)
            put(ja_ref, jb_ref, g, groups, y.astype(BF16))
        cross = lax.dot_general(q, p, nt, preferred_element_type=F32)
        hold[s, g] = jnp.where(same, cross, 0.0).astype(BF16)
    for s, g in every:
        x = hold[s, g]
        hold[s, g] = (mm(l_ref[s, g, 0], x) + mm(l_ref[s, g, 1], x)).astype(BF16)
    for g in range(groups):
        dense = []
        for s in range(2):
            x = hold[s, g]
            full = mm(x, r_ref[s, g, 0]) + mm(x, r_ref[s, g, 1])
            full = (full - jnp.transpose(full)) * (-2.0 * norm)
            dense.append(full[:n] + full[n : 2 * n] + full[2 * n : 3 * n] + full[3 * n :])
        out_ref[g * n : (g + 1) * n, :] = jnp.where(u < v, dense[0], dense[1])
    size = keep_ref.shape[0]
    y0 = y0_ref[0]
    keep_ref[...] = out_ref[pl.ds(pl.multiple_of(y0 * size, 8), size), :]
    send_ref[...] = out_ref[pl.ds(pl.multiple_of((1 - y0) * size, 8), size), :]


def unpack_kernel(y0_ref, mine_ref, other_ref, dep_ref, out_ref, packed, planes):
    size = mine_ref.shape[0]
    y0 = y0_ref[0]
    packed[pl.ds(pl.multiple_of(y0 * size, 8), size), :] = mine_ref[...]
    packed[pl.ds(pl.multiple_of((1 - y0) * size, 8), size), :] = other_ref[...]
    n = out_ref.shape[1]
    groups = packed.shape[0] // n
    for u in range(n):
        x = jnp.transpose(packed[pl.ds(u, groups, stride=n), :])
        planes[u * n : (u + 1) * n, :] = jnp.concatenate([x[q * n : (q + 1) * n] for q in range(GROUP)], 1)
    v = lax.broadcasted_iota(jnp.int32, (n, planes.shape[1]), 0)
    for u in range(n):
        x = planes[u * n : (u + 1) * n, :]
        y = planes[pl.ds(u, n, stride=n), :]
        out_ref[0, u] = jnp.where(v > u, x, 0.0) - jnp.where(v < u, y, 0.0)
        out_ref[1, u] = jnp.where(v < u, x, 0.0) - jnp.where(v > u, y, 0.0)


def gather_kernel(a_ref, b_ref, c_ref, d_ref, dep_ref, out_ref):
    for i, ref in enumerate((a_ref, b_ref, c_ref, d_ref)):
        out_ref[i] = ref[...]


def hidden_kernel(at_ref, own_ref, r1, r2, r3, core_ref, w_ref, keep_ref, send_ref, x_all):
    size = own_ref.shape[1]
    rows = w_ref.shape[0] // STEPS
    zi, xi, ci = at_ref[0], at_ref[1], at_ref[2]
    for d in range(4):
        src = (own_ref, r1, r2, r3)[d]
        for r in range(4):
            place = ((zi ^ r) * 4 + (xi + 4 - d) % 4) * 2
            x_all[pl.ds(pl.multiple_of((place + ci) * size, 16), size), :] = src[r]
            x_all[pl.ds(pl.multiple_of((place + 1 - ci) * size, 16), size), :] = core_ref[d, r]
    upper = zi >= 2
    for i in range(STEPS):
        y = mm(w_ref[i * rows : (i + 1) * rows, :], x_all[...]).astype(BF16)
        y = y.reshape(-1, 2, 16, y.shape[1])
        first, second = y[:, 0].reshape(-1, y.shape[3]), y[:, 1].reshape(-1, y.shape[3])
        span = slice(i * (rows // 2), (i + 1) * (rows // 2))
        keep_ref[span, :] = jnp.where(upper, second, first)
        send_ref[span, :] = jnp.where(upper, first, second)


def hidden_halves(place, own, r1, r2, r3, core, weight):
    rows, depth = weight.shape
    cols = own.shape[-1]
    shape = jax.ShapeDtypeStruct((rows // 2, cols), BF16)
    return pl.pallas_call(
        hidden_kernel,
        out_shape=(shape, shape),
        in_specs=[SMEM] + [VMEM] * 6,
        out_specs=(VMEM, VMEM),
        scratch_shapes=[
            pltpu.VMEM((depth, cols), BF16),
        ],
        compiler_params=WEIGHT_PARAMS,
        cost_estimate=cost(6),
        name="hidden",
    )(place, own, r1, r2, r3, core, weight)


def input_kernel(at_ref, own_ref, other_ref, w_ref, dep_ref, keep_ref, send_ref, gt, y_all):
    depth = w_ref.shape[1] // STEPS
    zi, xi, ci = at_ref[0], at_ref[1], at_ref[2]
    upper = zi >= 2
    a, b = own_ref[...], other_ref[...]
    cols = a.shape[1]
    first = jnp.where(upper, b, a).reshape(-1, 1, 16, cols)
    second = jnp.where(upper, a, b).reshape(-1, 1, 16, cols)
    whole = jnp.concatenate([first, second], 1).reshape(-1, cols)
    gt[...] = jnp.transpose(whole)
    size = keep_ref.shape[2]
    for z in range(STEPS):
        y_all[...] = jnp.transpose(mm(gt[...], w_ref[:, z * depth : (z + 1) * depth]))
        for d in range(4):
            spot = ((xi + d) % 4) * 2
            keep_ref[d, z ^ zi] = y_all[pl.ds(pl.multiple_of((spot + ci) * size, 16), size), :]
            send_ref[d, z ^ zi] = y_all[pl.ds(pl.multiple_of((spot + 1 - ci) * size, 16), size), :].astype(BF16)


def input_parts(place, own, other, weight, after):
    rows, depth = weight.shape
    cols = own.shape[-1]
    dims = (4, 4, depth // 32, cols)
    return pl.pallas_call(
        input_kernel,
        out_shape=(jax.ShapeDtypeStruct(dims, F32), jax.ShapeDtypeStruct(dims, BF16)),
        in_specs=[SMEM] + [VMEM] * 3 + [ANY],
        out_specs=(VMEM, VMEM),
        scratch_shapes=[
            pltpu.VMEM((cols, rows), BF16),
            pltpu.VMEM((depth // STEPS, cols), F32),
        ],
        compiler_params=WEIGHT_PARAMS,
        cost_estimate=cost(6),
        name="input_sums",
    )(place, own, other, weight, after)


def fold_kernel(keep_ref, rec_ref, dep_ref, own_ref, *send_refs):
    own_ref[...] = keep_ref[0] + rec_ref[0].astype(F32)
    for d, ref in enumerate(send_refs):
        ref[...] = (keep_ref[d + 1] + rec_ref[d + 1].astype(F32)).astype(BF16)


def fold(keep, rec, after):
    piece = keep.shape[1:]
    return pl.pallas_call(
        fold_kernel,
        out_shape=(jax.ShapeDtypeStruct(piece, F32),) + (jax.ShapeDtypeStruct(piece, BF16),) * 3,
        in_specs=[VMEM] * 2 + [ANY],
        out_specs=(VMEM,) * 4,
        compiler_params=PARAMS,
        cost_estimate=cost(1),
        name="fold",
    )(keep, rec, after)


def fold_last_kernel(own_ref, a_ref, b_ref, c_ref, keep_ref, *send_refs):
    for k in range(4):
        y = own_ref[k] + a_ref[k].astype(F32) + b_ref[k].astype(F32) + c_ref[k].astype(F32)
        if k == 0:
            keep_ref[...] = y
        else:
            send_refs[k - 1][...] = y.astype(BF16)


def fold_last(own, a, b, c):
    piece = own.shape[1:]
    return pl.pallas_call(
        fold_last_kernel,
        out_shape=(jax.ShapeDtypeStruct(piece, F32),) + (jax.ShapeDtypeStruct(piece, BF16),) * 3,
        in_specs=[VMEM] * 4,
        out_specs=(VMEM,) * 4,
        compiler_params=PARAMS,
        cost_estimate=cost(1),
        name="fold_last",
    )(own, a, b, c)


def load_kernel(w_hbm, dep_ref, out_ref, sem):
    copy = pltpu.make_async_copy(w_hbm, out_ref, sem)
    copy.start()
    copy.wait()


def load(weight, after):
    return pl.pallas_call(
        load_kernel,
        out_shape=jax.ShapeDtypeStruct(weight.shape, weight.dtype),
        in_specs=[HBM, ANY],
        out_specs=VMEM,
        scratch_shapes=[pltpu.SemaphoreType.DMA(())],
        compiler_params=WEIGHT_PARAMS,
        cost_estimate=cost(4),
        name="load",
    )(weight, after)


def add_kernel(a_ref, b_ref, dep_ref, out_ref):
    out_ref[...] = a_ref[...] + b_ref[...]


def add(a, b, after):
    return pl.pallas_call(
        add_kernel,
        out_shape=jax.ShapeDtypeStruct(a.shape, a.dtype),
        in_specs=[VMEM] * 2 + [ANY],
        out_specs=VMEM,
        compiler_params=PARAMS,
        cost_estimate=cost(0.2),
        name="add",
    )(a, b, after)


def join_kernel(at_ref, own_ref, other_ref, out_ref):
    high = at_ref[0] % 2 == 1
    a, b = own_ref[...], other_ref[...]
    cols = a.shape[1]
    first = jnp.where(high, b, a).reshape(-1, 1, 16, cols)
    second = jnp.where(high, a, b).reshape(-1, 1, 16, cols)
    out_ref[...] = jnp.concatenate([first, second], 1).reshape(-1, cols)


A_PAIRS = [(0, 0), (1, 2), (2, 1), (3, 3)]
B_PAIRS = [(0, 2), (1, 0), (2, 3), (3, 1)]
B_BACK = [(b, a) for a, b in B_PAIRS]


def per_device(responses, weight, skew, section_perm, prefix_ids, prefix_scale, out_grad):
    zi, xi, ci = lax.axis_index("z"), lax.axis_index("x"), lax.axis_index("c")
    yi = lax.axis_index("y")
    q = lax.bitwise_and(zi, 1)
    place = jnp.stack([zi, xi, ci]).astype(jnp.int32)
    n = skew.shape[-1]
    width = GROUP * n
    cols = responses.shape[0]
    mine = responses.T
    along_z = jnp.stack([mine] + [xor(mine, "z", k) for k in (1, 2, 3)])
    g_send = lax.dynamic_index_in_dim(out_grad.reshape(-1, 2, 16, cols), 1 - q, 1, keepdims=False)
    g_rec = xor(g_send.reshape(-1, cols), "z", 1)
    scale_rec = xor(prefix_scale, "z", 1)
    x2 = shift(along_z, "x", 2)
    x1 = shift(along_z, "x", 1)
    x3 = shift(along_z, "x", 3)
    turned, mt1 = invert(place, section_perm, skew, (along_z,))
    ids = prefix_ids[None, :]
    ga_out, gb_out = cotangent(place, out_grad, g_rec, prefix_scale, scale_rec, ids, mt1, along_z)
    ga = lax.ppermute(ga_out, "z", A_PAIRS)
    gb = lax.ppermute(gb_out, "z", B_BACK)
    by_x = pl.pallas_call(
        gather_kernel,
        out_shape=jax.ShapeDtypeStruct((4,) + along_z.shape, BF16),
        in_specs=[VMEM] * 4 + [ANY],
        out_specs=VMEM,
        compiler_params=PARAMS,
        cost_estimate=cost(1),
        name="gather",
    )(along_z, x1, x2, x3, ga_out)
    by_core = xor(by_x, "c", 1)
    z_own, z_send = hidden_halves(place, along_z, x1, x2, x3, by_core, weight)
    z_rec = xor(z_send, "z", 2)
    m0, mt0, m1, left, right = build(place, section_perm, turned, z_send)
    held = load(weight, z_send)
    h_own, h_send = turn(ga, gb, mt0, (held,))
    h_rec = xor(h_send, "z", 2)
    za_out, zb = turn(z_own, z_rec, m0, (h_send,))
    za = lax.ppermute(za_out, "z", A_PAIRS)
    zb = lax.ppermute(zb, "z", B_PAIRS)
    keep, send = input_parts(place, h_own, h_rec, held, za_out)
    send_rec = xor(send, "c", 1)
    rows_all = cols * lax.axis_size("y") * lax.axis_size("h")
    groups = left.shape[1]
    y0 = lax.bitwise_and(yi, 1).reshape(1)
    part_of = jax.ShapeDtypeStruct((groups * n // 2, width), F32)
    half_of = jax.ShapeDtypeStruct(za.shape, BF16)
    j_own, j_send, half, half_send = pl.pallas_call(
        functools.partial(last_kernel, 1.0 / rows_all**0.5),
        out_shape=(half_of, half_of, part_of, part_of),
        in_specs=[SMEM] * 2 + [VMEM] * 14 + [ANY],
        out_specs=(VMEM,) * 4,
        scratch_shapes=[
            pltpu.VMEM((2, groups, width, width), BF16),
            pltpu.VMEM((groups * n, width), F32),
            pltpu.VMEM(za.shape, F32),
            pltpu.VMEM(za.shape, F32),
        ],
        compiler_params=PARAMS,
        cost_estimate=cost(30),
        name="last",
    )(
        place, y0, out_grad, g_rec, prefix_scale, scale_rec, ids,
        m1, za, zb, ga, gb, z_own, z_rec, left, right, send,
    )
    j_rec = xor(j_send, "z", 1)
    judged = pl.pallas_call(
        join_kernel,
        out_shape=jax.ShapeDtypeStruct(out_grad.shape, BF16),
        in_specs=[SMEM] + [VMEM] * 2,
        out_specs=VMEM,
        compiler_params=PARAMS,
        cost_estimate=cost(0.01),
        name="join",
    )(place, j_own, j_rec)
    own, to1, to2, to3 = fold(keep, send_rec, half_send)
    half = half + xor(half_send, "y", 1)
    ours, z1, z2, z3 = fold_last(own, shift(to2, "x", 2), shift(to1, "x", 1), shift(to3, "x", 3))
    half = add(half, xor(half, "y", 2), pltpu.with_memory_space_constraint(judged, pltpu.HBM))
    half = add(half, xor(half, "h", 1), ours)
    final = ours + sum(xor(part, "z", k).astype(F32) for k, part in ((1, z1), (2, z2), (3, z3)))
    input_grad = final.astype(BF16)
    other = xor(half, "y", 1)
    skew_grad = pl.pallas_call(
        unpack_kernel,
        out_shape=jax.ShapeDtypeStruct((2, n, n, GROUP * groups), F32),
        in_specs=[SMEM] + [VMEM] * 2 + [ANY],
        out_specs=VMEM,
        scratch_shapes=[
            pltpu.VMEM((groups * n, width), F32),
            pltpu.VMEM((n * n, GROUP * groups), F32),
        ],
        compiler_params=PARAMS,
        cost_estimate=cost(0.01),
        name="unpack",
    )(y0, half, other, input_grad)
    return judged, input_grad, jnp.transpose(skew_grad, (0, 3, 1, 2))


def solution(mesh):
    wide = Mesh(mesh.devices.reshape(4, 2, 4, 4, 2), ("y", "h", "z", "x", "c"))
    dp, mp = ("y", "h"), ("z", "x", "c")
    in_specs = (
        P(dp, mp),
        P(mp, None),
        P(None, mp, None, None),
        P(),
        P(dp),
        P(None, mp),
        P(mp, dp),
    )
    out_specs = (P(mp, dp), P(mp, dp), P(None, mp, None, None))
    return jax.shard_map(per_device, mesh=wide, in_specs=in_specs, out_specs=out_specs, check_vma=False)
```

```python
import functools

import jax
import jax.numpy as jnp
from jax import lax
from jax.experimental import pallas as pl
from jax.experimental.pallas import tpu as pltpu
from jax.sharding import Mesh, PartitionSpec as P

F32 = jnp.float32
BF16 = jnp.bfloat16
GROUP = 4
VMEM_LIMIT = 12 * 1024 * 1024
WEIGHT_LIMIT = 20 * 1024 * 1024

VMEM = pl.BlockSpec(memory_space=pltpu.VMEM)
SMEM = pl.BlockSpec(memory_space=pltpu.SMEM)
ANY = pl.BlockSpec(memory_space=pl.ANY)
HBM = pl.BlockSpec(memory_space=pltpu.HBM)
PARAMS = pltpu.CompilerParams(vmem_limit_bytes=VMEM_LIMIT)
WEIGHT_PARAMS = pltpu.CompilerParams(vmem_limit_bytes=WEIGHT_LIMIT)
STEPS = 4


def cost(us):
    return pl.CostEstimate(flops=int(us * 1.15e9), bytes_accessed=0, transcendentals=0)


def xor(x, axis, k):
    return lax.ppermute(x, axis, [(i, i ^ k) for i in range(lax.axis_size(axis))])


def shift(x, axis, k):
    n = lax.axis_size(axis)
    return lax.ppermute(x, axis, [(i, (i + k) % n) for i in range(n)])


def mm(a, b):
    return jnp.dot(a, b, preferred_element_type=F32)


def split(x):
    hi = x.astype(BF16)
    return hi, (x - hi.astype(F32)).astype(BF16)


def eliminated(k_ref, mat, raw):
    n = k_ref.shape[1]
    blocks = k_ref.shape[3]
    raw[...] = jnp.zeros_like(raw)
    for s in range(2):
        raw[:, 64 * s : 64 * s + blocks] = k_ref[s].reshape(n * n, blocks)
    sub = lax.broadcasted_iota(jnp.int32, (n, 128), 0)
    for u in range(n):
        mat[u * n : (u + 1) * n, :] = (
            raw[u * n : (u + 1) * n, :] - raw[pl.ds(u, n, stride=n), :]
            + jnp.where(sub == u, 1.0, 0.0)
        )

    def eliminate(k, carry):
        at = sub == k
        base = pl.multiple_of(k * n, n)
        pivot = 1.0 / mat[pl.ds(base + k, 1), :]
        row = jnp.where(at, 1.0, mat[pl.ds(base, n), :]) * pivot
        for i in range(n):
            factor = mat[pl.ds(i * n + k, 1), :]
            mine = jnp.where(at, 0.0, mat[i * n : (i + 1) * n, :])
            mat[i * n : (i + 1) * n, :] = mine - factor * row
        mat[pl.ds(base, n), :] = row
        return carry

    lax.fori_loop(0, n, eliminate, 0)


def one_hots(at_ref, perm_ref, s, n):
    width = GROUP * n
    r = lax.broadcasted_iota(jnp.int32, (width, width), 0)
    c = lax.broadcasted_iota(jnp.int32, (width, width), 1)
    half = width // 2
    by_row, by_col = jnp.zeros_like(r), jnp.zeros_like(c)
    for u in range(n):
        by_row = jnp.where(r % n == u, perm_ref[s, u], by_row)
        by_col = jnp.where(c % n == u, perm_ref[s, u], by_col)

    def one_hot(raw_at, target, cut_at, bit):
        spot = ((cut_at // half) ^ bit) * 16 + cut_at % 16
        hit = (target == spot) & (raw_at // n == (cut_at // 16) % GROUP)
        return jnp.where(hit, 1.0, 0.0).astype(BF16)

    pi = one_hot(r, by_row, c, at_ref[0] // 2)
    pot = one_hot(c, by_col, r, at_ref[0] % 2)
    return pi, pot, r // n == c // n


def wide_block(turned, s, g, groups, n, diagonal):
    rows = [turned[pl.ds(64 * s + g + groups * q, n, stride=128), :] for q in range(GROUP)]
    return jnp.where(diagonal, jnp.concatenate([jnp.concatenate(rows, 0)] * GROUP, 1), 0.0)


def invert_kernel(at_ref, perm_ref, k_ref, *rest):
    turned, mt_ref, mat, raw = rest[-4:]
    eliminated(k_ref, mat, raw)
    n = k_ref.shape[1]
    groups = mt_ref.shape[0]
    for u in range(n):
        turned[u * 128 : (u + 1) * 128, :] = jnp.transpose(mat[u * n : (u + 1) * n, :])
    pi, pot, diagonal = one_hots(at_ref, perm_ref, 1, n)
    ident = mm(pot, pi)
    for g in range(groups):
        hi, lo = split(wide_block(turned, 1, g, groups, n, diagonal))
        rot = mm(pot, mm(hi, pi).astype(BF16)) + mm(pot, mm(lo, pi).astype(BF16))
        mt_ref[g, 0], mt_ref[g, 1] = split(jnp.transpose(2.0 * rot - ident))


def build_kernel(at_ref, perm_ref, turned, dep_ref, m0_ref, mt0_ref, m1_ref, l_ref, r_ref):
    groups = l_ref.shape[1]
    n = l_ref.shape[-1] // GROUP
    for s in range(2):
        pi, pot, diagonal = one_hots(at_ref, perm_ref, s, n)
        ident = mm(pot, pi)
        for g in range(groups):
            hi, lo = split(wide_block(turned, s, g, groups, n, diagonal))
            right_hi, right_lo = mm(hi, pi), mm(lo, pi)
            left = mm(pot, hi) + mm(pot, lo)
            l_ref[s, g, 0], l_ref[s, g, 1] = split(jnp.transpose(left))
            r_ref[s, g, 0], r_ref[s, g, 1] = split(jnp.transpose(right_hi + right_lo))
            rot = mm(pot, right_hi.astype(BF16)) + mm(pot, right_lo.astype(BF16))
            rot = 2.0 * rot - ident
            m_ref = m1_ref if s else m0_ref
            m_ref[g, 0], m_ref[g, 1] = split(rot)
            if s == 0:
                mt0_ref[g, 0], mt0_ref[g, 1] = split(jnp.transpose(rot))


def invert(place, section_perm, skew, after):
    n = skew.shape[-1]
    groups = skew.shape[1] // GROUP
    width = GROUP * n
    return pl.pallas_call(
        invert_kernel,
        out_shape=(
            jax.ShapeDtypeStruct((n * 128, n), F32),
            jax.ShapeDtypeStruct((groups, 2, width, width), BF16),
        ),
        in_specs=[SMEM] * 2 + [VMEM] + [ANY] * len(after),
        out_specs=(VMEM, VMEM),
        scratch_shapes=[pltpu.VMEM((n * n, 128), F32), pltpu.VMEM((n * n, 128), F32)],
        compiler_params=PARAMS,
        cost_estimate=cost(7),
        name="invert",
    )(place, section_perm, jnp.transpose(skew, (0, 2, 3, 1)), *after)


def build(place, section_perm, turned, after):
    n = turned.shape[1]
    groups = after.shape[0] // (16 * GROUP)
    width = GROUP * n
    one = jax.ShapeDtypeStruct((groups, 2, width, width), BF16)
    two = jax.ShapeDtypeStruct((2, groups, 2, width, width), BF16)
    return pl.pallas_call(
        build_kernel,
        out_shape=(one, one, one, two, two),
        in_specs=[SMEM] * 2 + [VMEM, ANY],
        out_specs=(VMEM,) * 5,
        compiler_params=PARAMS,
        cost_estimate=cost(5),
        name="build",
    )(place, section_perm, turned, after)


def spans(g, groups):
    return [slice(16 * (g + groups * q), 16 * (g + groups * q + 1)) for q in range(GROUP)]


def both(a_ref, b_ref, g, groups):
    rows = spans(g, groups)
    return jnp.concatenate([a_ref[row, :] for row in rows] + [b_ref[row, :] for row in rows], 0)


def put(oa_ref, ob_ref, g, groups, y):
    half = y.shape[0] // 2
    for q, row in enumerate(spans(g, groups)):
        oa_ref[row, :] = y[16 * q : 16 * (q + 1)]
        ob_ref[row, :] = y[half + 16 * q : half + 16 * (q + 1)]


def turn_kernel(a_ref, b_ref, m_ref, *rest):
    oa_ref, ob_ref = rest[-2:]
    groups = m_ref.shape[0]
    for g in range(groups):
        x = both(a_ref, b_ref, g, groups)
        y = mm(m_ref[g, 0], x) + mm(m_ref[g, 1], x)
        put(oa_ref, ob_ref, g, groups, y.astype(BF16))


def turn(a, b, m, after):
    shape = jax.ShapeDtypeStruct(a.shape, BF16)
    return pl.pallas_call(
        turn_kernel,
        out_shape=(shape, shape),
        in_specs=[VMEM] * 3 + [ANY] * len(after),
        out_specs=(VMEM, VMEM),
        compiler_params=PARAMS,
        cost_estimate=cost(1),
        name="turn",
    )(a, b, m, *after)


def scale_rows(ps_ref, ids, high):
    table = jnp.transpose(ps_ref[...])
    parts = []
    for _ in range(3):
        hi, _rest = split(table)
        parts.append(hi)
        table = table - hi.astype(F32)
    wanted = lax.broadcasted_iota(jnp.int32, (3 * ps_ref.shape[0], ids.shape[1]), 0) % ps_ref.shape[0]
    onehot = jnp.where(ids == wanted, 1.0, 0.0).astype(BF16)
    whole = mm(jnp.concatenate(parts, 1), onehot).reshape(-1, 2, 16, ids.shape[1])
    return jnp.where(high, whole[:, 1], whole[:, 0]).reshape(-1, ids.shape[1])


def scaled_cotangent(high, grad_ref, rec_ref, sa_ref, sb_ref, g, groups):
    rows = spans(g, groups)
    own = [grad_ref[2 * row.start : 2 * row.stop, :].reshape(2, 16, -1) for row in rows]
    own = [jnp.where(high, x[1], x[0]) for x in own]
    x = jnp.concatenate(own + [rec_ref[row, :] for row in rows], 0).astype(F32)
    return x * both(sa_ref, sb_ref, g, groups)


def cotangent_kernel(at_ref, grad_ref, rec_ref, mine_ref, theirs_ref, ids_ref, mt_ref, *rest):
    oa_ref, ob_ref, sa_ref, sb_ref = rest[1:]
    high = at_ref[0] % 2 == 1
    ids = ids_ref[...]
    sa_ref[...] = scale_rows(mine_ref, ids, high)
    sb_ref[...] = scale_rows(theirs_ref, ids, high)
    groups = mt_ref.shape[0]
    for g in range(groups):
        hi, lo = split(scaled_cotangent(high, grad_ref, rec_ref, sa_ref, sb_ref, g, groups))
        y = mm(mt_ref[g, 0], hi) + (mm(mt_ref[g, 1], hi) + mm(mt_ref[g, 0], lo))
        put(oa_ref, ob_ref, g, groups, y.astype(BF16))


def cotangent(place, out_grad, rec, mine, theirs, ids, mt, after):
    shape = jax.ShapeDtypeStruct(rec.shape, BF16)
    return pl.pallas_call(
        cotangent_kernel,
        out_shape=(shape, shape),
        in_specs=[SMEM] + [VMEM] * 6 + [ANY],
        out_specs=(VMEM, VMEM),
        scratch_shapes=[pltpu.VMEM(rec.shape, F32)] * 2,
        compiler_params=PARAMS,
        cost_estimate=cost(3),
        name="cotangent",
    )(place, out_grad, rec, mine, theirs, ids, mt, after)


def last_kernel(norm, at_ref, y0_ref, grad_ref, rec_ref, mine_ref, theirs_ref, ids_ref, *rest):
    (m_ref, p1a, p1b, q0a, q0b, p0a, p0b, l_ref, r_ref, dep_ref) = rest[:10]
    (ja_ref, jb_ref, keep_ref, send_ref, hold, out_ref, sa_ref, sb_ref) = rest[10:]
    high = at_ref[0] % 2 == 1
    ids = ids_ref[...]
    sa_ref[...] = scale_rows(mine_ref, ids, high)
    sb_ref[...] = scale_rows(theirs_ref, ids, high)
    groups = l_ref.shape[1]
    width = l_ref.shape[-1]
    n = width // GROUP
    r = lax.broadcasted_iota(jnp.int32, (width, width), 0)
    c = lax.broadcasted_iota(jnp.int32, (width, width), 1)
    same = (r // 16) % GROUP == (c // 16) % GROUP
    u = lax.broadcasted_iota(jnp.int32, (n, width), 0)
    v = lax.broadcasted_iota(jnp.int32, (n, width), 1) % n
    nt = (((1,), (1,)), ((), ()))
    every = [(s, g) for s in range(2) for g in range(groups)]
    for s, g in every:
        if s == 0:
            q = both(q0a, q0b, g, groups)
            p = both(p0a, p0b, g, groups)
        else:
            q = scaled_cotangent(high, grad_ref, rec_ref, sa_ref, sb_ref, g, groups).astype(BF16)
            p = both(p1a, p1b, g, groups)
            y = (mm(m_ref[g, 0], p) + mm(m_ref[g, 1], p)) * both(sa_ref, sb_ref, g, groups)
            put(ja_ref, jb_ref, g, groups, y.astype(BF16))
        cross = lax.dot_general(q, p, nt, preferred_element_type=F32)
        hold[s, g] = jnp.where(same, cross, 0.0).astype(BF16)
    for s, g in every:
        x = hold[s, g]
        hold[s, g] = (mm(l_ref[s, g, 0], x) + mm(l_ref[s, g, 1], x)).astype(BF16)
    for g in range(groups):
        dense = []
        for s in range(2):
            x = hold[s, g]
            full = mm(x, r_ref[s, g, 0]) + mm(x, r_ref[s, g, 1])
            full = (full - jnp.transpose(full)) * (-2.0 * norm)
            dense.append(full[:n] + full[n : 2 * n] + full[2 * n : 3 * n] + full[3 * n :])
        out_ref[g * n : (g + 1) * n, :] = jnp.where(u < v, dense[0], dense[1])
    size = keep_ref.shape[0]
    y0 = y0_ref[0]
    keep_ref[...] = out_ref[pl.ds(pl.multiple_of(y0 * size, 8), size), :]
    send_ref[...] = out_ref[pl.ds(pl.multiple_of((1 - y0) * size, 8), size), :]


def unpack_kernel(y0_ref, mine_ref, other_ref, dep_ref, out_ref, packed, planes):
    size = mine_ref.shape[0]
    y0 = y0_ref[0]
    packed[pl.ds(pl.multiple_of(y0 * size, 8), size), :] = mine_ref[...]
    packed[pl.ds(pl.multiple_of((1 - y0) * size, 8), size), :] = other_ref[...]
    n = out_ref.shape[1]
    groups = packed.shape[0] // n
    for u in range(n):
        x = jnp.transpose(packed[pl.ds(u, groups, stride=n), :])
        planes[u * n : (u + 1) * n, :] = jnp.concatenate([x[q * n : (q + 1) * n] for q in range(GROUP)], 1)
    v = lax.broadcasted_iota(jnp.int32, (n, planes.shape[1]), 0)
    for u in range(n):
        x = planes[u * n : (u + 1) * n, :]
        y = planes[pl.ds(u, n, stride=n), :]
        out_ref[0, u] = jnp.where(v > u, x, 0.0) - jnp.where(v < u, y, 0.0)
        out_ref[1, u] = jnp.where(v < u, x, 0.0) - jnp.where(v > u, y, 0.0)


def gather_kernel(a_ref, b_ref, c_ref, d_ref, dep_ref, out_ref):
    for i, ref in enumerate((a_ref, b_ref, c_ref, d_ref)):
        out_ref[i] = ref[...]


def hidden_kernel(at_ref, own_ref, r1, r2, r3, core_ref, w_ref, keep_ref, send_ref, x_all):
    size = own_ref.shape[1]
    rows = w_ref.shape[0] // STEPS
    zi, xi, ci = at_ref[0], at_ref[1], at_ref[2]
    for d in range(4):
        src = (own_ref, r1, r2, r3)[d]
        for r in range(4):
            place = ((zi ^ r) * 4 + (xi + 4 - d) % 4) * 2
            x_all[pl.ds(pl.multiple_of((place + ci) * size, 16), size), :] = src[r]
            x_all[pl.ds(pl.multiple_of((place + 1 - ci) * size, 16), size), :] = core_ref[d, r]
    upper = zi >= 2
    for i in range(STEPS):
        y = mm(w_ref[i * rows : (i + 1) * rows, :], x_all[...]).astype(BF16)
        y = y.reshape(-1, 2, 16, y.shape[1])
        first, second = y[:, 0].reshape(-1, y.shape[3]), y[:, 1].reshape(-1, y.shape[3])
        span = slice(i * (rows // 2), (i + 1) * (rows // 2))
        keep_ref[span, :] = jnp.where(upper, second, first)
        send_ref[span, :] = jnp.where(upper, first, second)


def hidden_halves(place, own, r1, r2, r3, core, weight):
    rows, depth = weight.shape
    cols = own.shape[-1]
    shape = jax.ShapeDtypeStruct((rows // 2, cols), BF16)
    return pl.pallas_call(
        hidden_kernel,
        out_shape=(shape, shape),
        in_specs=[SMEM] + [VMEM] * 6,
        out_specs=(VMEM, VMEM),
        scratch_shapes=[
            pltpu.VMEM((depth, cols), BF16),
        ],
        compiler_params=WEIGHT_PARAMS,
        cost_estimate=cost(6),
        name="hidden",
    )(place, own, r1, r2, r3, core, weight)


def input_kernel(at_ref, own_ref, other_ref, w_ref, dep_ref, keep_ref, send_ref, gt, y_all):
    depth = w_ref.shape[1] // STEPS
    zi, xi, ci = at_ref[0], at_ref[1], at_ref[2]
    upper = zi >= 2
    a, b = own_ref[...], other_ref[...]
    cols = a.shape[1]
    first = jnp.where(upper, b, a).reshape(-1, 1, 16, cols)
    second = jnp.where(upper, a, b).reshape(-1, 1, 16, cols)
    whole = jnp.concatenate([first, second], 1).reshape(-1, cols)
    gt[...] = jnp.transpose(whole)
    size = keep_ref.shape[2]
    for z in range(STEPS):
        y_all[...] = jnp.transpose(mm(gt[...], w_ref[:, z * depth : (z + 1) * depth]))
        for d in range(4):
            spot = ((xi + d) % 4) * 2
            keep_ref[d, z ^ zi] = y_all[pl.ds(pl.multiple_of((spot + ci) * size, 16), size), :]
            send_ref[d, z ^ zi] = y_all[pl.ds(pl.multiple_of((spot + 1 - ci) * size, 16), size), :].astype(BF16)


def input_parts(place, own, other, weight, after):
    rows, depth = weight.shape
    cols = own.shape[-1]
    dims = (4, 4, depth // 32, cols)
    return pl.pallas_call(
        input_kernel,
        out_shape=(jax.ShapeDtypeStruct(dims, F32), jax.ShapeDtypeStruct(dims, BF16)),
        in_specs=[SMEM] + [VMEM] * 3 + [ANY],
        out_specs=(VMEM, VMEM),
        scratch_shapes=[
            pltpu.VMEM((cols, rows), BF16),
            pltpu.VMEM((depth // STEPS, cols), F32),
        ],
        compiler_params=WEIGHT_PARAMS,
        cost_estimate=cost(6),
        name="input_sums",
    )(place, own, other, weight, after)


def fold_kernel(keep_ref, rec_ref, dep_ref, own_ref, *send_refs):
    own_ref[...] = keep_ref[0] + rec_ref[0].astype(F32)
    for d, ref in enumerate(send_refs):
        ref[...] = (keep_ref[d + 1] + rec_ref[d + 1].astype(F32)).astype(BF16)


def fold(keep, rec, after):
    piece = keep.shape[1:]
    return pl.pallas_call(
        fold_kernel,
        out_shape=(jax.ShapeDtypeStruct(piece, F32),) + (jax.ShapeDtypeStruct(piece, BF16),) * 3,
        in_specs=[VMEM] * 2 + [ANY],
        out_specs=(VMEM,) * 4,
        compiler_params=PARAMS,
        cost_estimate=cost(1),
        name="fold",
    )(keep, rec, after)


def fold_last_kernel(own_ref, a_ref, b_ref, c_ref, keep_ref, *send_refs):
    for k in range(4):
        y = own_ref[k] + a_ref[k].astype(F32) + b_ref[k].astype(F32) + c_ref[k].astype(F32)
        if k == 0:
            keep_ref[...] = y
        else:
            send_refs[k - 1][...] = y.astype(BF16)


def fold_last(own, a, b, c):
    piece = own.shape[1:]
    return pl.pallas_call(
        fold_last_kernel,
        out_shape=(jax.ShapeDtypeStruct(piece, F32),) + (jax.ShapeDtypeStruct(piece, BF16),) * 3,
        in_specs=[VMEM] * 4,
        out_specs=(VMEM,) * 4,
        compiler_params=PARAMS,
        cost_estimate=cost(1),
        name="fold_last",
    )(own, a, b, c)


def load_kernel(w_hbm, dep_ref, out_ref, sem):
    copy = pltpu.make_async_copy(w_hbm, out_ref, sem)
    copy.start()
    copy.wait()


def load(weight, after):
    return pl.pallas_call(
        load_kernel,
        out_shape=jax.ShapeDtypeStruct(weight.shape, weight.dtype),
        in_specs=[HBM, ANY],
        out_specs=VMEM,
        scratch_shapes=[pltpu.SemaphoreType.DMA(())],
        compiler_params=WEIGHT_PARAMS,
        cost_estimate=cost(4),
        name="load",
    )(weight, after)


def add_kernel(a_ref, b_ref, dep_ref, out_ref):
    out_ref[...] = a_ref[...] + b_ref[...]


def add(a, b, after):
    return pl.pallas_call(
        add_kernel,
        out_shape=jax.ShapeDtypeStruct(a.shape, a.dtype),
        in_specs=[VMEM] * 2 + [ANY],
        out_specs=VMEM,
        compiler_params=PARAMS,
        cost_estimate=cost(0.2),
        name="add",
    )(a, b, after)


def join_kernel(at_ref, own_ref, other_ref, out_ref):
    high = at_ref[0] % 2 == 1
    a, b = own_ref[...], other_ref[...]
    cols = a.shape[1]
    first = jnp.where(high, b, a).reshape(-1, 1, 16, cols)
    second = jnp.where(high, a, b).reshape(-1, 1, 16, cols)
    out_ref[...] = jnp.concatenate([first, second], 1).reshape(-1, cols)


A_PAIRS = [(0, 0), (1, 2), (2, 1), (3, 3)]
B_PAIRS = [(0, 2), (1, 0), (2, 3), (3, 1)]
B_BACK = [(b, a) for a, b in B_PAIRS]


def per_device(responses, weight, skew, section_perm, prefix_ids, prefix_scale, out_grad):
    zi, xi, ci = lax.axis_index("z"), lax.axis_index("x"), lax.axis_index("c")
    yi = lax.axis_index("y")
    q = lax.bitwise_and(zi, 1)
    place = jnp.stack([zi, xi, ci]).astype(jnp.int32)
    n = skew.shape[-1]
    width = GROUP * n
    cols = responses.shape[0]
    mine = responses.T
    along_z = jnp.stack([mine] + [xor(mine, "z", k) for k in (1, 2, 3)])
    g_send = lax.dynamic_index_in_dim(out_grad.reshape(-1, 2, 16, cols), 1 - q, 1, keepdims=False)
    g_rec = xor(g_send.reshape(-1, cols), "z", 1)
    scale_rec = xor(prefix_scale, "z", 1)
    x2 = shift(along_z, "x", 2)
    x1 = shift(along_z, "x", 1)
    x3 = shift(along_z, "x", 3)
    turned, mt1 = invert(place, section_perm, skew, (along_z,))
    ids = prefix_ids[None, :]
    ga_out, gb_out = cotangent(place, out_grad, g_rec, prefix_scale, scale_rec, ids, mt1, along_z)
    ga = lax.ppermute(ga_out, "z", A_PAIRS)
    gb = lax.ppermute(gb_out, "z", B_BACK)
    by_x = pl.pallas_call(
        gather_kernel,
        out_shape=jax.ShapeDtypeStruct((4,) + along_z.shape, BF16),
        in_specs=[VMEM] * 4 + [ANY],
        out_specs=VMEM,
        compiler_params=PARAMS,
        cost_estimate=cost(1),
        name="gather",
    )(along_z, x1, x2, x3, ga_out)
    by_core = xor(by_x, "c", 1)
    z_own, z_send = hidden_halves(place, along_z, x1, x2, x3, by_core, weight)
    z_rec = xor(z_send, "z", 2)
    m0, mt0, m1, left, right = build(place, section_perm, turned, z_send)
    h_own, h_send = turn(ga, gb, mt0, (z_send,))
    held = load(pltpu.with_memory_space_constraint(weight, pltpu.HBM), h_send)
    h_rec = xor(h_send, "z", 2)
    za_out, zb = turn(z_own, z_rec, m0, (held,))
    za = lax.ppermute(za_out, "z", A_PAIRS)
    zb = lax.ppermute(zb, "z", B_PAIRS)
    keep, send = input_parts(place, h_own, h_rec, held, za_out)
    send_rec = xor(send, "c", 1)
    rows_all = cols * lax.axis_size("y") * lax.axis_size("h")
    groups = left.shape[1]
    y0 = lax.bitwise_and(yi, 1).reshape(1)
    part_of = jax.ShapeDtypeStruct((groups * n // 2, width), F32)
    half_of = jax.ShapeDtypeStruct(za.shape, BF16)
    j_own, j_send, half, half_send = pl.pallas_call(
        functools.partial(last_kernel, 1.0 / rows_all**0.5),
        out_shape=(half_of, half_of, part_of, part_of),
        in_specs=[SMEM] * 2 + [VMEM] * 14 + [ANY],
        out_specs=(VMEM,) * 4,
        scratch_shapes=[
            pltpu.VMEM((2, groups, width, width), BF16),
            pltpu.VMEM((groups * n, width), F32),
            pltpu.VMEM(za.shape, F32),
            pltpu.VMEM(za.shape, F32),
        ],
        compiler_params=PARAMS,
        cost_estimate=cost(30),
        name="last",
    )(
        place, y0, out_grad, g_rec, prefix_scale, scale_rec, ids,
        m1, za, zb, ga, gb, z_own, z_rec, left, right, send,
    )
    j_rec = xor(j_send, "z", 1)
    judged = pl.pallas_call(
        join_kernel,
        out_shape=jax.ShapeDtypeStruct(out_grad.shape, BF16),
        in_specs=[SMEM] + [VMEM] * 2,
        out_specs=VMEM,
        compiler_params=PARAMS,
        cost_estimate=cost(0.01),
        name="join",
    )(place, j_own, j_rec)
    own, to1, to2, to3 = fold(keep, send_rec, za_out)
    half = half + xor(half_send, "y", 1)
    ours, z1, z2, z3 = fold_last(own, shift(to2, "x", 2), shift(to1, "x", 1), shift(to3, "x", 3))
    half = add(half, xor(half, "y", 2), pltpu.with_memory_space_constraint(judged, pltpu.HBM))
    half = add(half, xor(half, "h", 1), ours)
    final = ours + sum(xor(part, "z", k).astype(F32) for k, part in ((1, z1), (2, z2), (3, z3)))
    input_grad = final.astype(BF16)
    other = xor(half, "y", 1)
    skew_grad = pl.pallas_call(
        unpack_kernel,
        out_shape=jax.ShapeDtypeStruct((2, n, n, GROUP * groups), F32),
        in_specs=[SMEM] + [VMEM] * 2 + [ANY],
        out_specs=VMEM,
        scratch_shapes=[
            pltpu.VMEM((groups * n, width), F32),
            pltpu.VMEM((n * n, GROUP * groups), F32),
        ],
        compiler_params=PARAMS,
        cost_estimate=cost(0.01),
        name="unpack",
    )(y0, half, other, input_grad)
    return judged, input_grad, jnp.transpose(skew_grad, (0, 3, 1, 2))


def solution(mesh):
    wide = Mesh(mesh.devices.reshape(4, 2, 4, 4, 2), ("y", "h", "z", "x", "c"))
    dp, mp = ("y", "h"), ("z", "x", "c")
    in_specs = (
        P(dp, mp),
        P(mp, None),
        P(None, mp, None, None),
        P(),
        P(dp),
        P(None, mp),
        P(mp, dp),
    )
    out_specs = (P(mp, dp), P(mp, dp), P(None, mp, None, None))
    return jax.shard_map(per_device, mesh=wide, in_specs=in_specs, out_specs=out_specs, check_vma=False)
```
